256 devices in a mesh: gy: 64 (over z, y, core), gz: 4 (over x).
Axes of the slice: x: 4, y: 4, z: 8, core: 2. Of those that a mesh axis runs over, the one named last changes fastest.
Arguments:
- field: bfloat16 [32, 8, 1024, 1024], P(None, None, 'gy', 'gz'), may hold values from -6 to 6
- spectral_weight: bfloat16 [256, 32, 1024], P('gy', 'gz'), may hold values from -1 to 1
- point_weight: bfloat16 [32, 32], replicated, may hold values from -1 to 1
- bias: float32 [32], replicated, may hold values from -3 to 3
Outputs:
- layer_out: bfloat16 [32, 8, 1024, 1024], P(None, None, 'gy', 'gz')
The draws below stay inside these ranges and needn't reach their ends.
All inputs are finite; a program needn't handle non-finite values.
Results may differ from the reference program's by a relative error of at most 0.013.
Values may be sent and summed in bfloat16 or wider, within the bound.
No kernel may reach another device: no remote copies, remote signals or barrier semaphores. Data moves between devices by JAX's collectives and lax.ppermute only.
A program may use at most 64 MiB of HBM per device.

```python
import math
import jax
import jax.numpy as jnp
from jax import lax

C = 32
KY = 32
KZ = 32
X = 8
KX = 8
NY = 1024
NZ = 1024


def steps_of(own_key, dims, split, least, high):
    loudness = 1.0
    for axis_at, blocks in split:
        heights = jax.random.uniform(jax.random.fold_in(jax.random.fold_in(own_key, 6), axis_at), (blocks,), jnp.float32, least / len(split), high / len(split))
        loudness = loudness * jnp.repeat(jnp.exp(heights), dims[axis_at] // blocks).reshape((-1,) + (1,) * (len(dims) - 1 - axis_at))
    return loudness


def normal_values(key, shape, spread, most, pieces=(), held_as=jnp.bfloat16):
    level = steps_of(key, shape, pieces, -0.22, 0.18) if pieces else 1.0
    entries = jax.random.normal(key, shape, jnp.float32) * spread * level
    return jnp.minimum(jnp.maximum(entries, -most), most).astype(held_as)


def setup_inputs(seed: int = 0) -> dict:
    arg_keys = jax.random.split(jax.random.key(seed), 5)
    return {
        "field": normal_values(arg_keys[0], (C, X, NY, NZ), 1.0, 6.0, ((2, 64), (3, 4))),
        "spectral_weight": normal_values(arg_keys[1], (KX * KY, KZ, C * C), C ** -0.5, 1.0, ((0, 64), (1, 4))),
        "point_weight": normal_values(arg_keys[2], (C, C), C ** -0.5, 1.0),
        "bias": normal_values(arg_keys[3], (C,), 0.5, 3.0, (), jnp.float32),
    }


def basis(count, length, start, size, norm):
    modes = jnp.arange(count, dtype=jnp.float32)[:, None]
    spots = (start + lax.iota(jnp.int32, size)).astype(jnp.float32)[None, :]
    value = norm * jnp.cos(jnp.pi * modes * (spots + 0.5) / length)
    return jnp.where(modes == 0, value * math.sqrt(0.5), value)

def reference(field, spectral_weight, point_weight, bias):
    highest = lax.Precision.HIGHEST
    block = math.gcd(NY, 64)
    indices = jnp.arange(NY // block, dtype=jnp.int32)
    rounded_z = basis(KZ, NZ, 0, NZ, math.sqrt(2.0 / NZ)).astype(jnp.bfloat16)
    analysis_z = lax.optimization_barrier(rounded_z).astype(jnp.float32)
    analysis_y = basis(KY, NY, 0, NY, math.sqrt(2.0 / NY))
    analysis_x = basis(KX, X, 0, X, math.sqrt(2.0 / X))

    def forward(carry, index):
        piece = lax.dynamic_slice_in_dim(field, index * block, block, 2).astype(jnp.float32)
        part = jnp.einsum('cxyz,kz->cxyk', piece, analysis_z, precision=highest)
        rows_basis = lax.dynamic_slice_in_dim(analysis_y, index * block, block, 1)
        return (carry + jnp.einsum('cxyk,jy->cxjk', part, rows_basis, precision=highest), None)
    start = jnp.zeros((C, X, KY, KZ), jnp.float32)
    summed, unused = lax.scan(forward, start, indices)
    spectrum = jnp.einsum('cxjk,ix->cijk', summed, analysis_x, precision=highest)
    weight = spectral_weight.astype(jnp.float32).reshape(KX, KY, KZ, C, C)
    mixed = jnp.einsum('cijk,ijkco->oijk', spectrum, weight, precision=highest).astype(jnp.bfloat16)
    mixed = lax.optimization_barrier(mixed).astype(jnp.float32)
    synth_x = basis(KX, X, 0, X, math.sqrt(2.0 / KX))
    synth_y = basis(KY, NY, 0, NY, math.sqrt(2.0 / KY))
    synth_z = basis(KZ, NZ, 0, NZ, math.sqrt(2.0 / KZ))
    modes_x = jnp.einsum('cijk,ix->cxjk', mixed, synth_x, precision=highest)
    point = point_weight.astype(jnp.float32)
    shift = bias.astype(jnp.float32)[:, None, None, None]

    def backward(index):
        piece = lax.dynamic_slice_in_dim(field, index * block, block, 2).astype(jnp.float32)
        rows_basis = lax.dynamic_slice_in_dim(synth_y, index * block, block, 1)
        spatial = jnp.einsum('cxjk,jy->cxyk', modes_x, rows_basis, precision=highest)
        spatial = jnp.einsum('cxyk,kz->cxyz', spatial, synth_z, precision=highest)
        local = jnp.einsum('cxyz,co->oxyz', piece, point, precision=highest)
        return jax.nn.gelu(spatial + local + shift, approximate=True).astype(jnp.bfloat16)
    blocks = lax.map(backward, indices)
    return jnp.moveaxis(blocks, 0, 2).reshape(C, X, NY, NZ)
```

```python
import math

import jax
import jax.numpy as jnp
import ml_dtypes
import numpy as np
from jax import lax
from jax.experimental import pallas as pl
from jax.experimental.pallas import tpu as pltpu
from jax.sharding import Mesh
from jax.sharding import PartitionSpec as P

C, X, K, N = 32, 8, 32, 1024
DZ, DY, DC, DX = 8, 4, 2, 4
ROWS = N // (DZ * DY * DC)
DEPTH = N // DX
BF = jnp.bfloat16
F32 = jnp.float32


def cosines(count, length, norm):
    modes = np.arange(count, dtype=np.float64)[:, None]
    spots = np.arange(length, dtype=np.float64)[None, :]
    value = norm * np.cos(np.pi * modes * (spots + 0.5) / length)
    value[0] *= math.sqrt(0.5)
    return value


def tables():
    ax = cosines(X, X, math.sqrt(2.0 / X))
    ay = cosines(K, N, math.sqrt(2.0 / N))
    az = cosines(K, N, math.sqrt(2.0 / N)).astype(ml_dtypes.bfloat16).astype(np.float64)
    sz = cosines(K, N, math.sqrt(2.0 / K))
    kq, kx, i = np.meshgrid(np.arange(4), np.arange(DX), np.arange(X), indexing="ij")
    front = np.zeros((DX, X, DC, 128, DEPTH))
    for core in range(DC):
        k = (kx * 8 + core * 4 + kq).reshape(-1)
        rows = az[k].reshape(128, DX, DEPTH).transpose(1, 0, 2)
        mixx = ax[i.reshape(-1)]
        front[:, :, core] = rows[:, None] * mixx.T[None, :, :, None]
    along = np.zeros((DZ * DY * DC, 32, 32))
    for dev in range(DZ * DY * DC):
        core = dev % 2
        spots = np.concatenate([dev * ROWS + np.arange(ROWS), (dev ^ 1) * ROWS + np.arange(ROWS)])
        octet = np.concatenate([core * 4 + np.arange(4), (1 - core) * 4 + np.arange(4)])
        j = (np.arange(4)[:, None] * 8 + octet[None, :]).reshape(-1)
        along[dev] = ay[j][:, spots].T
    back = np.zeros((DX * DC, 48, DEPTH))
    q2, x2 = np.meshgrid(np.arange(4), np.arange(DX), indexing="ij")
    for chip in range(DX):
        for core in range(DC):
            own = (x2 * 8 + core * 4 + q2).reshape(-1)
            other = (x2 * 8 + (1 - core) * 4 + q2).reshape(-1)
            part = slice(chip * DEPTH, (chip + 1) * DEPTH)
            back[chip * 2 + core, :16] = sz[own][:, part]
            back[chip * 2 + core, 16:32] = sz[other][:, part]
            back[chip * 2 + core, 32:35] = 1.0
    planes = np.zeros((X, 16, 16, X))
    for m in range(16):
        planes[:, m, m, :] = ax.T * math.sqrt(N / K)
    bf = ml_dtypes.bfloat16
    return (
        front.astype(bf),
        along.astype(bf),
        back.astype(bf),
        planes.reshape(128, 128).astype(bf),
    )


def dot(a, b, dims=((1,), (0,))):
    return lax.dot_general(a, b, (dims, ((), ())), preferred_element_type=F32)


def iota(shape, dim):
    return lax.broadcasted_iota(jnp.int32, shape, dim)


def ones_where(condition):
    return jnp.where(condition, 1.0, 0.0).astype(BF)


def tables_kernel(at_ref, along_ref, point_ref, bias_ref, wy_ref, kron_ref, shift_ref, spread_ref):
    p1 = ones_where(
        (iota((512, 32), 0) // 256 == iota((512, 32), 1) // 16)
        & (iota((512, 32), 0) % 16 == iota((512, 32), 1) % 16)
    )
    p2 = ones_where(
        (iota((32, 512), 0) // 8 == iota((32, 512), 1) // 128)
        & (iota((32, 512), 0) % 8 == iota((32, 512), 1) % 8)
    )
    full = dot(dot(p1, along_ref[0]).astype(BF), p2)
    same = (iota((512, 512), 0) // 16) % 16 == (iota((512, 512), 1) // 8) % 16
    wy_ref[...] = jnp.where(same, full, 0.0).astype(BF)
    e1 = ones_where(iota((512, 32), 0) // 16 == iota((512, 32), 1))
    e2 = ones_where(iota((32, 512), 0) == iota((32, 512), 1) // 16)
    wide = dot(dot(e1, point_ref[...], ((1,), (1,))).astype(BF), e2)
    same = iota((512, 512), 0) % 16 == iota((512, 512), 1) % 16
    kron_ref[...] = jnp.where(same, wide, 0.0).astype(BF)
    b = jnp.broadcast_to(bias_ref[...], (16, 32))
    b1 = b.astype(BF).astype(F32)
    b2 = (b - b1).astype(BF).astype(F32)
    b3 = b - b1 - b2
    row = iota((16, 32), 0)
    parts = jnp.where(row == 0, b1, jnp.where(row == 1, b2, jnp.where(row == 2, b3, 0.0)))
    shift_ref[...] = dot(parts.astype(BF), e2).astype(BF)
    spread_ref[...] = ones_where(iota((256, 1024), 0) // 8 == iota((256, 1024), 1) // 32)


def analysis_kernel(at_ref, field_ref, mine_ref, other_ref, own_ref, send_ref, acc0, acc1):
    plane = field_ref[...].reshape(C * ROWS, DEPTH)
    a0 = dot(mine_ref[0, 0, 0], plane, ((1,), (1,)))
    a1 = dot(other_ref[0, 0, 0], plane, ((1,), (1,)))
    step = pl.program_id(0)

    @pl.when(step == 0)
    def _():
        acc0[...] = a0
        acc1[...] = a1

    @pl.when(step > 0)
    def _():
        acc0[...] += a0
        acc1[...] += a1

    @pl.when(step == X - 1)
    def _():
        own_ref[...] = acc0[...].astype(BF)
        send_ref[...] = acc1[...].astype(BF)


def rows_kernel(own_ref, recv_ref, wy_ref, out_ref, scratch):
    for g in range(2):
        half = pl.ds(g * 256, 256)
        lhs = jnp.concatenate([own_ref[:, half], recv_ref[:, half]], axis=1)
        res = dot(lhs, wy_ref[...])
        for kq in range(4):
            for kx in range(4):
                for joct in range(4):
                    start = (kx * 4 + joct) * 64 + g * 4 + kq
                    first = (kq * 4 + kx) * 8
                    scratch[pl.ds(start, 8, stride=8), :] = res[
                        first : first + 8, joct * 128 : (joct + 1) * 128
                    ]
    out_ref[...] = scratch[...].astype(BF)


def mix_kernel(at_ref, parts_ref, weight_ref, peer_ref, spread_ref, out_ref):
    core = at_ref[0]
    s = jnp.sum(parts_ref[...].astype(F32).reshape(128, 8, 128), axis=0)
    row = iota((8, 128), 0)
    turned = pltpu.roll(s, 4, 0)
    s8 = jnp.concatenate([jnp.where(row < 4, s, turned), jnp.where(row < 4, turned, s)], axis=1)
    s64 = jnp.concatenate([s8] * 8, axis=0)
    row = iota((64, 256), 0)
    keep = (iota((64, 256), 1) % 8 == row // 8) & ((row % 8) // 4 == core)
    s64 = jnp.where(keep, s64, 0.0)
    high = s64.astype(BF)
    low = (s64 - high.astype(F32)).astype(BF)
    spread = spread_ref[...]
    wide = dot(high, spread) + dot(low, spread)
    weight = jnp.concatenate(
        [weight_ref[...].astype(F32).reshape(32, 1024), peer_ref[...].astype(F32).reshape(32, 1024)], axis=0
    )
    prod = wide * weight
    total = prod[:, 0:128]
    for part in range(1, 8):
        total = total + prod[:, part * 128 : (part + 1) * 128]
    total = total + pltpu.roll(total, 64, 1)
    total = total + pltpu.roll(total, 32, 1)
    mixed = total.astype(BF)
    q, col = iota((128, 256), 0), iota((128, 256), 1)
    place = ones_where(q == (col // 128) * 16 + (col % 128) // 8)
    placed = dot(mixed, place)
    placed = jnp.where(iota((64, 256), 1) % 8 == iota((64, 256), 0) // 8, placed, 0.0).astype(BF)
    take = ones_where(iota((8, 64), 0) % 4 == iota((8, 64), 1) % 4)
    both = dot(take, placed)
    out = jnp.where(iota((8, 128), 0) < 4, both[:, :128], both[:, 128:])
    out_ref[...] = jnp.broadcast_to(out[None], (128, 8, 128)).reshape(1024, 128).astype(BF)


def modes_kernel(modes_ref, wy_ref, planes_ref, own_ref, send_ref, scratch):
    scratch[...] = modes_ref[...].astype(F32)
    for g in range(2):
        cols = []
        for joct in range(4):
            pieces = []
            for kq in range(4):
                for kx in range(4):
                    start = (kx * 4 + joct) * 64 + g * 4 + kq
                    pieces.append(scratch[pl.ds(start, 8, stride=8), :])
            cols.append(jnp.concatenate(pieces, axis=0))
        lhs = jnp.concatenate(cols, axis=1).astype(BF)
        res = dot(lhs, wy_ref[...], ((1,), (1,))).astype(BF)
        res = dot(planes_ref[...], res).astype(BF)
        half = pl.ds(g * 256, 256)
        own_ref[:, half] = res[:, :256]
        send_ref[:, half] = res[:, 256:]


def grid_kernel(at_ref, field_ref, kron_ref, own_ref, recv_ref, shift_ref, back_ref, out_ref):
    plane = field_ref[...].reshape(C * ROWS, DEPTH)
    modes = jnp.concatenate([own_ref[...], recv_ref[...], shift_ref[...]], axis=0)
    v = dot(kron_ref[...], plane) + dot(modes, back_ref[0], ((0,), (0,)))
    a = math.sqrt(2.0 / math.pi)
    inner = v * (a + (a * 0.044715) * (v * v))
    half = 0.5 * v
    out_ref[...] = (half + half * jnp.tanh(inner)).astype(BF).reshape(C, 1, ROWS, DEPTH)


def shards(field, spectral_weight, point_weight, bias):
    front, along, back, planes = (jnp.asarray(t) for t in tables())
    chip = lax.axis_index("x")
    core = lax.axis_index("c")
    rows_at = (lax.axis_index("z") * DY + lax.axis_index("y")) * DC + core
    at = jnp.stack([core, chip, rows_at]).astype(jnp.int32)
    swap = [(0, 1), (1, 0)]
    bf = lambda *shape: jax.ShapeDtypeStruct(shape, BF)
    full = lambda *shape: pl.BlockSpec(shape, lambda *_: (0,) * len(shape))

    peer_weight = lax.ppermute(spectral_weight, "c", swap)

    own, send = pl.pallas_call(
        analysis_kernel,
        out_shape=(bf(128, 512), bf(128, 512)),
        grid_spec=pltpu.PrefetchScalarGridSpec(
            num_scalar_prefetch=1,
            grid=(X,),
            in_specs=[
                pl.BlockSpec((C, 1, ROWS, DEPTH), lambda x, at: (0, x, 0, 0)),
                pl.BlockSpec((1, 1, 1, 128, DEPTH), lambda x, at: (at[1], x, at[0], 0, 0)),
                pl.BlockSpec((1, 1, 1, 128, DEPTH), lambda x, at: (at[1], x, 1 - at[0], 0, 0)),
            ],
            out_specs=[full(128, 512), full(128, 512)],
            scratch_shapes=[pltpu.VMEM((128, 512), F32)] * 2,
        ),
        name="analysis",
    )(at, field, front, front)

    wy, kron, shift, spread = pl.pallas_call(
        tables_kernel,
        out_shape=(bf(512, 512), bf(512, 512), bf(16, 512), bf(256, 1024)),
        grid_spec=pltpu.PrefetchScalarGridSpec(
            num_scalar_prefetch=1,
            grid=(1,),
            in_specs=[
                pl.BlockSpec((1, 32, 32), lambda _, at: (at[2], 0, 0)),
                full(32, 32),
                full(1, 32),
            ],
            out_specs=[full(512, 512), full(512, 512), full(16, 512), full(256, 1024)],
        ),
        name="tables",
    )(at, along, point_weight, bias.reshape(1, 32))

    recv = lax.ppermute(send, "c", swap)
    parts = pl.pallas_call(
        rows_kernel,
        out_shape=bf(1024, 128),
        scratch_shapes=[pltpu.VMEM((1024, 128), F32)],
        name="rows",
    )(own, recv, wy)
    parts = lax.all_to_all(parts.reshape(128, 8, 128), ("x", "y", "z"), 0, 0, tiled=True)

    mixed = pl.pallas_call(
        mix_kernel,
        out_shape=bf(1024, 128),
        grid_spec=pltpu.PrefetchScalarGridSpec(
            num_scalar_prefetch=1,
            grid=(1,),
            in_specs=[full(1024, 128), full(4, 8, 1024), full(4, 8, 1024), full(256, 1024)],
            out_specs=full(1024, 128),
        ),
        name="mix",
    )(at, parts.reshape(1024, 128), spectral_weight, peer_weight, spread)
    modes = lax.all_to_all(mixed.reshape(128, 8, 128), ("x", "y", "z"), 0, 0, tiled=True)

    own, send = pl.pallas_call(
        modes_kernel,
        out_shape=(bf(128, 512), bf(128, 512)),
        scratch_shapes=[pltpu.VMEM((1024, 128), F32)],
        name="modes",
    )(modes.reshape(1024, 128), wy, planes)
    recv = lax.ppermute(send, "c", swap)

    return pl.pallas_call(
        grid_kernel,
        out_shape=bf(C, X, ROWS, DEPTH),
        grid_spec=pltpu.PrefetchScalarGridSpec(
            num_scalar_prefetch=1,
            grid=(X,),
            in_specs=[
                pl.BlockSpec((C, 1, ROWS, DEPTH), lambda x, at: (0, x, 0, 0)),
                full(512, 512),
                pl.BlockSpec((16, 512), lambda x, at: (x, 0)),
                pl.BlockSpec((16, 512), lambda x, at: (x, 0)),
                full(16, 512),
                pl.BlockSpec((1, 48, DEPTH), lambda x, at: (at[1] * 2 + at[0], 0, 0)),
            ],
            out_specs=pl.BlockSpec((C, 1, ROWS, DEPTH), lambda x, at: (0, x, 0, 0)),
        ),
        name="grid",
    )(at, field, kron, own, recv, shift, back)


def solution(mesh):
    fine = Mesh(mesh.devices.reshape(DZ, DY, DC, DX), ("z", "y", "c", "x"))
    return jax.shard_map(
        shards,
        mesh=fine,
        in_specs=(P(None, None, ("z", "y", "c"), "x"), P(("z", "y", "c"), "x", None), P(), P()),
        out_specs=P(None, None, ("z", "y", "c"), "x"),
        check_vma=False,
    )
```

```python
import math

import jax
import jax.numpy as jnp
import ml_dtypes
import numpy as np
from jax import lax
from jax.experimental import pallas as pl
from jax.experimental.pallas import tpu as pltpu
from jax.sharding import Mesh
from jax.sharding import PartitionSpec as P

C, X, K, N = 32, 8, 32, 1024
DZ, DY, DC, DX = 8, 4, 2, 4
ROWS = N // (DZ * DY * DC)
DEPTH = N // DX
CHUNKS = 4
BF = jnp.bfloat16
F32 = jnp.float32


def cosines(count, length, norm):
    modes = np.arange(count, dtype=np.float64)[:, None]
    spots = np.arange(length, dtype=np.float64)[None, :]
    value = norm * np.cos(np.pi * modes * (spots + 0.5) / length)
    value[0] *= math.sqrt(0.5)
    return value


def tables():
    ax = cosines(X, X, math.sqrt(2.0 / X))
    ay = cosines(K, N, math.sqrt(2.0 / N))
    az = cosines(K, N, math.sqrt(2.0 / N)).astype(ml_dtypes.bfloat16).astype(np.float64)
    sz = cosines(K, N, math.sqrt(2.0 / K))
    kq, kx, i = np.meshgrid(np.arange(4), np.arange(DX), np.arange(X), indexing="ij")
    front = np.zeros((DX, DC, DEPTH, 2, 128))
    for core in range(DC):
        for h in range(2):
            k = (kx * 8 + (core ^ h) * 4 + kq).reshape(-1)
            front[:, core, :, h] = az[k].reshape(128, DX, DEPTH).transpose(1, 2, 0)
    across = np.tile(ax[i.reshape(-1)].T, (1, 2))
    along = np.zeros((DZ * DY * DC, 32, 32))
    for dev in range(DZ * DY * DC):
        core = dev % 2
        spots = np.concatenate([dev * ROWS + np.arange(ROWS), (dev ^ 1) * ROWS + np.arange(ROWS)])
        octet = np.concatenate([core * 4 + np.arange(4), (1 - core) * 4 + np.arange(4)])
        j = (np.arange(4)[:, None] * 8 + octet[None, :]).reshape(-1)
        along[dev] = ay[j][:, spots].T
    back = np.zeros((DX * DC, 48, DEPTH))
    q2, x2 = np.meshgrid(np.arange(4), np.arange(DX), indexing="ij")
    for chip in range(DX):
        for core in range(DC):
            own = (x2 * 8 + core * 4 + q2).reshape(-1)
            other = (x2 * 8 + (1 - core) * 4 + q2).reshape(-1)
            part = slice(chip * DEPTH, (chip + 1) * DEPTH)
            back[chip * 2 + core, :16] = sz[own][:, part]
            back[chip * 2 + core, 16:32] = sz[other][:, part]
            back[chip * 2 + core, 32:35] = 1.0
    planes = np.zeros((X, 16, 16, X))
    for m in range(16):
        planes[:, m, m, :] = ax.T * math.sqrt(N / K)
    bf = ml_dtypes.bfloat16
    return (
        front.reshape(DX, DC, DEPTH, 256).astype(bf),
        across.astype(np.float32),
        along.astype(bf),
        back.astype(bf),
        planes.reshape(128, 128).astype(bf),
    )


def dot(a, b, dims=((1,), (0,))):
    return lax.dot_general(a, b, (dims, ((), ())), preferred_element_type=F32)


def iota(shape, dim):
    return lax.broadcasted_iota(jnp.int32, shape, dim)


def ones_where(condition):
    return jnp.where(condition, 1.0, 0.0).astype(BF)


def at_chip():
    return lax.axis_index("x")


def at_core():
    return lax.axis_index("c")


def at_rows():
    return (lax.axis_index("z") * DY + lax.axis_index("y")) * DC + lax.axis_index("c")


def analysis_kernel(
    field, front, across, along, own, send, wy, grid, weights, base, vectors, piece, field_sem, sems
):
    loads = [
        pltpu.make_async_copy(front.at[at_chip(), at_core()], base, sems.at[0]),
        pltpu.make_async_copy(across, vectors, sems.at[1]),
        pltpu.make_async_copy(along.at[at_rows()], piece, sems.at[2]),
    ]
    for load in loads:
        load.start()
    copy = pltpu.make_async_copy(field, grid, field_sem)
    copy.start()
    for load in loads:
        load.wait()
    wide = base[...].astype(F32)
    for x in range(X):
        weights[pl.ds(x * DEPTH, DEPTH), :] = (wide * vectors[pl.ds(x, 1), :]).astype(BF)
    p1 = ones_where(
        (iota((512, 32), 0) // 256 == iota((512, 32), 1) // 16)
        & (iota((512, 32), 0) % 16 == iota((512, 32), 1) % 16)
    )
    p2 = ones_where(
        (iota((32, 512), 0) // 8 == iota((32, 512), 1) // 128)
        & (iota((32, 512), 0) % 8 == iota((32, 512), 1) % 8)
    )
    same = (iota((512, 512), 0) // 16) % 16 == (iota((512, 512), 1) // 8) % 16
    full = dot(dot(p1, piece[...]).astype(BF), p2)
    wy[...] = jnp.where(same, full, 0.0).astype(BF)
    copy.wait()
    lhs = jnp.concatenate([grid[:, x].reshape(C * ROWS, DEPTH) for x in range(X)], axis=1)
    res = dot(lhs, weights[...]).T.astype(BF)
    own[...] = res[:128]
    send[...] = res[128:]


def tables_kernel(
    point_ref, bias_ref, back_ref, planes_ref, after_ref, kron_ref, shift_ref, spread_ref, back_out, planes_out, sems
):
    loads = [
        pltpu.make_async_copy(back_ref.at[at_chip() * DC + at_core()], back_out, sems.at[0]),
        pltpu.make_async_copy(planes_ref, planes_out, sems.at[1]),
    ]
    for load in loads:
        load.start()
    e1 = ones_where(iota((512, 32), 0) // 16 == iota((512, 32), 1))
    e2 = ones_where(iota((32, 512), 0) == iota((32, 512), 1) // 16)
    wide = dot(dot(e1, point_ref[...], ((1,), (1,))).astype(BF), e2)
    same = iota((512, 512), 0) % 16 == iota((512, 512), 1) % 16
    kron_ref[...] = jnp.where(same, wide, 0.0).astype(BF)
    b = jnp.broadcast_to(bias_ref[...], (16, 32))
    b1 = b.astype(BF).astype(F32)
    b2 = (b - b1).astype(BF).astype(F32)
    b3 = b - b1 - b2
    row = iota((16, 32), 0)
    parts = jnp.where(row == 0, b1, jnp.where(row == 1, b2, jnp.where(row == 2, b3, 0.0)))
    shift_ref[...] = dot(parts.astype(BF), e2).astype(BF)
    spread_ref[...] = ones_where(iota((128, 512), 0) // 8 == iota((128, 512), 1) // 32)
    for load in loads:
        load.wait()


def rows_kernel(own_ref, recv_ref, wy_ref, out_ref, scratch):
    for g in range(2):
        half = pl.ds(g * 256, 256)
        lhs = jnp.concatenate([own_ref[:, half], recv_ref[:, half]], axis=1)
        res = dot(lhs, wy_ref[...])
        for kq in range(4):
            for kx in range(4):
                for joct in range(4):
                    start = (kx * 4 + joct) * 64 + g * 4 + kq
                    first = (kq * 4 + kx) * 8
                    scratch[pl.ds(start, 8, stride=8), :] = res[
                        first : first + 8, joct * 128 : (joct + 1) * 128
                    ]
    out_ref[...] = scratch[...].astype(BF)


def mix_kernel(parts_ref, weight_ref, peer_ref, spread_ref, out_ref):
    core = at_core()
    s = jnp.sum(parts_ref[...].astype(F32).reshape(128, 8, 128), axis=0)
    row = iota((8, 128), 0)
    turned = pltpu.roll(s, 4, 0)
    s8 = jnp.concatenate([jnp.where(row < 4, s, turned), jnp.where(row < 4, turned, s)], axis=1)
    s64 = jnp.concatenate([s8] * 8, axis=0)
    row = iota((64, 256), 0)
    keep = (iota((64, 256), 1) % 8 == row // 8) & ((row % 8) // 4 == core)
    s64 = jnp.where(keep, s64, 0.0)
    high = s64.astype(BF)
    low = (s64 - high.astype(F32)).astype(BF)
    spread = spread_ref[...]
    halves = [dot(high[:, part], spread) + dot(low[:, part], spread) for part in (slice(0, 128), slice(128, 256))]
    wide = jnp.concatenate(halves, axis=1)
    weight = jnp.concatenate(
        [weight_ref[...].astype(F32).reshape(32, 1024), peer_ref[...].astype(F32).reshape(32, 1024)], axis=0
    )
    prod = wide * weight
    total = prod[:, 0:128]
    for part in range(1, 8):
        total = total + prod[:, part * 128 : (part + 1) * 128]
    total = total + pltpu.roll(total, 64, 1)
    total = total + pltpu.roll(total, 32, 1)
    mixed = total.astype(BF)
    q, col = iota((128, 256), 0), iota((128, 256), 1)
    place = ones_where(q == (col // 128) * 16 + (col % 128) // 8)
    placed = dot(mixed, place)
    placed = jnp.where(iota((64, 256), 1) % 8 == iota((64, 256), 0) // 8, placed, 0.0).astype(BF)
    take = ones_where(iota((8, 64), 0) % 4 == iota((8, 64), 1) % 4)
    both = dot(take, placed)
    out = jnp.where(iota((8, 128), 0) < 4, both[:, :128], both[:, 128:])
    out_ref[...] = jnp.broadcast_to(out[None], (128, 8, 128)).reshape(1024, 128).astype(BF)


def modes_kernel(modes_ref, wy_ref, planes_ref, after_ref, own_ref, send_ref, scratch):
    scratch[...] = modes_ref[...].astype(F32)
    for g in range(2):
        cols = []
        for joct in range(4):
            pieces = []
            for kq in range(4):
                for kx in range(4):
                    start = (kx * 4 + joct) * 64 + g * 4 + kq
                    pieces.append(scratch[pl.ds(start, 8, stride=8), :])
            cols.append(jnp.concatenate(pieces, axis=0))
        lhs = jnp.concatenate(cols, axis=1).astype(BF)
        res = dot(lhs, wy_ref[...], ((1,), (1,))).astype(BF)
        res = dot(planes_ref[...], res).astype(BF)
        half = pl.ds(g * 256, 256)
        own_ref[:, half] = res[:, :256]
        send_ref[:, half] = res[:, 256:]


def point_kernel(field, kron_ref, after_ref, out_ref, grid, sem):
    copy = pltpu.make_async_copy(field, grid, sem)
    copy.start()
    copy.wait()
    for x in range(X):
        out_ref[x] = dot(kron_ref[...], grid[:, x].reshape(C * ROWS, DEPTH)).astype(BF)


def grid_kernel(point_ref, own_ref, recv_ref, shift_ref, back_ref, out_ref, stage, sems):
    a = 2.0 * math.sqrt(2.0 / math.pi)
    share = C // CHUNKS
    copies = []
    for q in range(CHUNKS):
        cols = pl.ds(q * share * ROWS, share * ROWS)
        rows = pl.ds(q * share, share)
        for x in range(X):
            part = pl.ds(x * 16, 16)
            modes = jnp.concatenate([own_ref[part, cols], recv_ref[part, cols], shift_ref[:, cols]], axis=0)
            v = point_ref[x, cols, :].astype(F32) + dot(modes, back_ref[...], ((0,), (0,)))
            v = v * jax.nn.sigmoid(v * (a + (a * 0.044715) * (v * v)))
            stage[rows, x] = v.astype(BF).reshape(share, ROWS, DEPTH)
        copies.append(pltpu.make_async_copy(stage.at[rows], out_ref.at[rows], sems.at[q]))
        copies[-1].start()
    for copy in copies:
        copy.wait()


def call(kernel, name, args, outs, scratch=(), spaces=None):
    spaces = spaces or [pltpu.VMEM] * len(args)
    args = [x if s is pl.ANY else pltpu.with_memory_space_constraint(x, s) for x, s in zip(args, spaces)]
    spec = lambda s: pl.BlockSpec(memory_space=pl.ANY if s is pltpu.HBM else s)
    return pl.pallas_call(
        kernel,
        out_shape=outs,
        in_specs=[spec(s) for s in spaces],
        out_specs=jax.tree.map(lambda o: spec(o.memory_space), outs),
        scratch_shapes=list(scratch),
        compiler_params=pltpu.CompilerParams(vmem_limit_bytes=12 * 2**20),
        name=name,
    )(*args)


def shards(field, spectral_weight, point_weight, bias):
    front, across, along, back, planes = (jnp.asarray(t) for t in tables())
    swap = [(0, 1), (1, 0)]
    vm = lambda *shape, dtype=BF: pltpu.VMEM(shape, dtype)
    dma = pltpu.SemaphoreType.DMA

    peer_weight = lax.ppermute(spectral_weight, "c", swap)
    own, send, wy = call(
        analysis_kernel,
        "analysis",
        (field, front, across, along),
        (vm(128, 512), vm(128, 512), vm(512, 512)),
        (
            vm(C, X, ROWS, DEPTH),
            vm(X * DEPTH, 256),
            vm(DEPTH, 256),
            vm(X, 256, dtype=F32),
            vm(32, 32),
            dma,
            dma((3,)),
        ),
        (pltpu.HBM,) * 4,
    )
    recv = lax.ppermute(send, "c", swap)
    parts = call(rows_kernel, "rows", (own, recv, wy), vm(1024, 128), (vm(1024, 128, dtype=F32),))
    kron, shift, spread, back, planes = call(
        tables_kernel,
        "tables",
        (point_weight, bias.reshape(1, 32), back, planes, parts),
        (vm(512, 512), vm(16, 512), vm(128, 512), vm(48, DEPTH), vm(128, 128)),
        (dma((2,)),),
        (pltpu.VMEM, pltpu.VMEM, pltpu.HBM, pltpu.HBM, pl.ANY),
    )
    parts = lax.all_to_all(parts.reshape(128, 8, 128), ("x", "y", "z"), 0, 0, tiled=True)
    mixed = call(
        mix_kernel,
        "mix",
        (parts.reshape(1024, 128), spectral_weight, peer_weight, spread),
        vm(1024, 128),
    )
    point = call(
        point_kernel,
        "point",
        (field, kron, mixed),
        vm(X, C * ROWS, DEPTH),
        (vm(C, X, ROWS, DEPTH), dma),
        (pltpu.HBM, pltpu.VMEM, pl.ANY),
    )
    modes = lax.all_to_all(mixed.reshape(128, 8, 128), ("x", "y", "z"), 0, 0, tiled=True)
    own, send = call(
        modes_kernel,
        "modes",
        (modes.reshape(1024, 128), wy, planes, point),
        (vm(128, 512), vm(128, 512)),
        (vm(1024, 128, dtype=F32),),
        (pltpu.VMEM, pltpu.VMEM, pltpu.VMEM, pl.ANY),
    )
    recv = lax.ppermute(send, "c", swap)
    return call(
        grid_kernel,
        "grid",
        (point, own, recv, shift, back),
        pltpu.HBM((C, X, ROWS, DEPTH), BF),
        (vm(C, X, ROWS, DEPTH), dma((CHUNKS,))),
    )


def solution(mesh):
    fine = Mesh(mesh.devices.reshape(DZ, DY, DC, DX), ("z", "y", "c", "x"))
    return jax.shard_map(
        shards,
        mesh=fine,
        in_specs=(P(None, None, ("z", "y", "c"), "x"), P(("z", "y", "c"), "x", None), P(), P()),
        out_specs=P(None, None, ("z", "y", "c"), "x"),
        check_vma=False,
    )
```

```python
import math

import jax
import jax.numpy as jnp
import ml_dtypes
import numpy as np
from jax import lax
from jax.experimental import pallas as pl
from jax.experimental.pallas import tpu as pltpu
from jax.sharding import Mesh
from jax.sharding import PartitionSpec as P

C, X, K, N = 32, 8, 32, 1024
DZ, DY, DC, DX = 8, 4, 2, 4
ROWS = N // (DZ * DY * DC)
DEPTH = N // DX
CHUNKS = 4
BF = jnp.bfloat16
F32 = jnp.float32


def cosines(count, length, norm):
    modes = np.arange(count, dtype=np.float64)[:, None]
    spots = np.arange(length, dtype=np.float64)[None, :]
    value = norm * np.cos(np.pi * modes * (spots + 0.5) / length)
    value[0] *= math.sqrt(0.5)
    return value


def tables():
    ax = cosines(X, X, math.sqrt(2.0 / X))
    ay = cosines(K, N, math.sqrt(2.0 / N))
    az = cosines(K, N, math.sqrt(2.0 / N)).astype(ml_dtypes.bfloat16).astype(np.float64)
    sz = cosines(K, N, math.sqrt(2.0 / K))
    kq, kx, i = np.meshgrid(np.arange(4), np.arange(DX), np.arange(X), indexing="ij")
    front = np.zeros((DX, DC, DEPTH, 2, 128))
    for core in range(DC):
        for h in range(2):
            k = (kx * 8 + (core ^ h) * 4 + kq).reshape(-1)
            front[:, core, :, h] = az[k].reshape(128, DX, DEPTH).transpose(1, 2, 0)
    across = np.tile(ax[i.reshape(-1)].T, (1, 2))
    along = np.zeros((DZ * DY * DC, 32, 32))
    for dev in range(DZ * DY * DC):
        core = dev % 2
        spots = np.concatenate([dev * ROWS + np.arange(ROWS), (dev ^ 1) * ROWS + np.arange(ROWS)])
        octet = np.concatenate([core * 4 + np.arange(4), (1 - core) * 4 + np.arange(4)])
        j = (np.arange(4)[:, None] * 8 + octet[None, :]).reshape(-1)
        along[dev] = ay[j][:, spots].T
    back = np.zeros((DX * DC, 48, DEPTH))
    q2, x2 = np.meshgrid(np.arange(4), np.arange(DX), indexing="ij")
    for chip in range(DX):
        for core in range(DC):
            own = (x2 * 8 + core * 4 + q2).reshape(-1)
            other = (x2 * 8 + (1 - core) * 4 + q2).reshape(-1)
            part = slice(chip * DEPTH, (chip + 1) * DEPTH)
            back[chip * 2 + core, :16] = sz[own][:, part]
            back[chip * 2 + core, 16:32] = sz[other][:, part]
            back[chip * 2 + core, 32:35] = 1.0
    planes = np.zeros((X, 16, 16, X))
    for m in range(16):
        planes[:, m, m, :] = ax.T * math.sqrt(N / K)
    bf = ml_dtypes.bfloat16
    return (
        front.reshape(DX, DC, DEPTH, 256).astype(bf),
        across.astype(np.float32),
        along.astype(bf),
        back.astype(bf),
        planes.reshape(128, 128).astype(bf),
    )


def dot(a, b, dims=((1,), (0,))):
    return lax.dot_general(a, b, (dims, ((), ())), preferred_element_type=F32)


def iota(shape, dim):
    return lax.broadcasted_iota(jnp.int32, shape, dim)


def ones_where(condition):
    return jnp.where(condition, 1.0, 0.0).astype(BF)


def at_chip():
    return lax.axis_index("x")


def at_core():
    return lax.axis_index("c")


def at_rows():
    return (lax.axis_index("z") * DY + lax.axis_index("y")) * DC + lax.axis_index("c")


def analysis_kernel(
    field, front, across, back, planes, own, send, back_out, planes_out, grid, weights, base, vectors, field_sem, sems
):
    loads = [
        pltpu.make_async_copy(front.at[at_chip(), at_core()], base, sems.at[0]),
        pltpu.make_async_copy(across, vectors, sems.at[1]),
        pltpu.make_async_copy(back.at[at_chip() * DC + at_core()], back_out, sems.at[2]),
        pltpu.make_async_copy(planes, planes_out, sems.at[3]),
    ]
    copy = pltpu.make_async_copy(field, grid, field_sem)
    loads[0].start()
    loads[1].start()
    copy.start()
    loads[2].start()
    loads[3].start()
    loads[0].wait()
    loads[1].wait()
    wide = base[...].astype(F32)
    for x in range(X):
        weights[pl.ds(x * DEPTH, DEPTH), :] = (wide * vectors[pl.ds(x, 1), :]).astype(BF)
    copy.wait()
    lhs = jnp.concatenate([grid[:, x].reshape(C * ROWS, DEPTH) for x in range(X)], axis=1)
    res = dot(lhs, weights[...]).T.astype(BF)
    own[...] = res[:128]
    send[...] = res[128:]
    loads[2].wait()
    loads[3].wait()


def tables_kernel(along, point_ref, bias_ref, wy, kron_ref, shift_ref, spread_ref, piece, sem):
    load = pltpu.make_async_copy(along.at[at_rows()], piece, sem)
    load.start()
    e1 = ones_where(iota((512, 32), 0) // 16 == iota((512, 32), 1))
    e2 = ones_where(iota((32, 512), 0) == iota((32, 512), 1) // 16)
    wide = dot(dot(e1, point_ref[...], ((1,), (1,))).astype(BF), e2)
    same = iota((512, 512), 0) % 16 == iota((512, 512), 1) % 16
    kron_ref[...] = jnp.where(same, wide, 0.0).astype(BF)
    b = jnp.broadcast_to(bias_ref[...], (16, 32))
    b1 = b.astype(BF).astype(F32)
    b2 = (b - b1).astype(BF).astype(F32)
    b3 = b - b1 - b2
    row = iota((16, 32), 0)
    parts = jnp.where(row == 0, b1, jnp.where(row == 1, b2, jnp.where(row == 2, b3, 0.0)))
    shift_ref[...] = dot(parts.astype(BF), e2).astype(BF)
    spread_ref[...] = ones_where(iota((128, 512), 0) // 8 == iota((128, 512), 1) // 32)
    p1 = ones_where(
        (iota((256, 32), 0) // 128 == iota((256, 32), 1) // 16)
        & (iota((256, 32), 0) % 16 == iota((256, 32), 1) % 16)
    )
    p2 = ones_where(
        (iota((32, 256), 0) // 8 == iota((32, 256), 1) // 64)
        & (iota((32, 256), 0) % 8 == iota((32, 256), 1) % 8)
    )
    same = (iota((256, 256), 0) // 16) % 8 == (iota((256, 256), 1) // 8) % 8
    load.wait()
    full = dot(dot(p1, piece[...]).astype(BF), p2)
    wy[...] = jnp.where(same, full, 0.0).astype(BF)


def rows_kernel(own_ref, recv_ref, wy_ref, after_ref, out_ref, scratch):
    blocks = []
    for e in range(4):
        part = pl.ds(e * 128, 128)
        blocks.append(dot(jnp.concatenate([own_ref[:, part], recv_ref[:, part]], axis=1), wy_ref[...]))
    for g in range(2):
        for joct in range(4):
            cols = slice(joct * 64, (joct + 1) * 64)
            res = jnp.concatenate([blocks[2 * g][:, cols], blocks[2 * g + 1][:, cols]], axis=1)
            for kq in range(4):
                for kx in range(4):
                    start = (kx * 4 + joct) * 64 + g * 4 + kq
                    first = (kq * 4 + kx) * 8
                    scratch[pl.ds(start, 8, stride=8), :] = res[first : first + 8, :]
    out_ref[...] = scratch[...].astype(BF)


def mix_kernel(parts_ref, weight_ref, peer_ref, spread_ref, out_ref):
    core = at_core()
    s = jnp.sum(parts_ref[...].astype(F32).reshape(128, 8, 128), axis=0)
    row = iota((8, 128), 0)
    turned = pltpu.roll(s, 4, 0)
    s8 = jnp.concatenate([jnp.where(row < 4, s, turned), jnp.where(row < 4, turned, s)], axis=1)
    s64 = jnp.concatenate([s8] * 8, axis=0)
    row = iota((64, 256), 0)
    keep = (iota((64, 256), 1) % 8 == row // 8) & ((row % 8) // 4 == core)
    s64 = jnp.where(keep, s64, 0.0)
    high = s64.astype(BF)
    low = (s64 - high.astype(F32)).astype(BF)
    spread = spread_ref[...]
    halves = [dot(high[:, part], spread) + dot(low[:, part], spread) for part in (slice(0, 128), slice(128, 256))]
    wide = jnp.concatenate(halves, axis=1)
    weight = jnp.concatenate(
        [weight_ref[...].astype(F32).reshape(32, 1024), peer_ref[...].astype(F32).reshape(32, 1024)], axis=0
    )
    prod = wide * weight
    total = prod[:, 0:128]
    for part in range(1, 8):
        total = total + prod[:, part * 128 : (part + 1) * 128]
    total = total + pltpu.roll(total, 64, 1)
    total = total + pltpu.roll(total, 32, 1)
    mixed = total.astype(BF)
    q, col = iota((128, 256), 0), iota((128, 256), 1)
    place = ones_where(q == (col // 128) * 16 + (col % 128) // 8)
    placed = dot(mixed, place)
    placed = jnp.where(iota((64, 256), 1) % 8 == iota((64, 256), 0) // 8, placed, 0.0).astype(BF)
    take = ones_where(iota((8, 64), 0) % 4 == iota((8, 64), 1) % 4)
    both = dot(take, placed)
    out = jnp.where(iota((8, 128), 0) < 4, both[:, :128], both[:, 128:])
    out_ref[...] = jnp.broadcast_to(out[None], (128, 8, 128)).reshape(1024, 128).astype(BF)


def modes_kernel(modes_ref, wy_ref, planes_ref, own_ref, send_ref, scratch):
    scratch[...] = modes_ref[...].astype(F32)
    for g in range(2):
        cols = []
        for joct in range(4):
            pieces = []
            for kq in range(4):
                for kx in range(4):
                    start = (kx * 4 + joct) * 64 + g * 4 + kq
                    pieces.append(scratch[pl.ds(start, 8, stride=8), :])
            cols.append(jnp.concatenate(pieces, axis=0))
        for e in range(2):
            lanes = slice(e * 64, (e + 1) * 64)
            lhs = jnp.concatenate([col[:, lanes] for col in cols], axis=1).astype(BF)
            res = dot(lhs, wy_ref[...], ((1,), (1,))).astype(BF)
            res = dot(planes_ref[...], res).astype(BF)
            part = pl.ds((g * 2 + e) * 128, 128)
            own_ref[:, part] = res[:, :128]
            send_ref[:, part] = res[:, 128:]


def point_kernel(grid_ref, kron_ref, after_ref, out_ref):
    for x in range(X):
        out_ref[x] = dot(kron_ref[...], grid_ref[:, x].reshape(C * ROWS, DEPTH))


def grid_kernel(point_ref, own_ref, recv_ref, shift_ref, back_ref, out_ref, stage, sems):
    a = 2.0 * math.sqrt(2.0 / math.pi)
    share = C // CHUNKS
    copies = []
    for q in range(CHUNKS):
        cols = pl.ds(q * share * ROWS, share * ROWS)
        rows = pl.ds(q * share, share)
        for x in range(X):
            part = pl.ds(x * 16, 16)
            modes = jnp.concatenate([own_ref[part, cols], recv_ref[part, cols], shift_ref[:, cols]], axis=0)
            v = point_ref[x, cols, :] + dot(modes, back_ref[...], ((0,), (0,)))
            v = v * jax.nn.sigmoid(v * (a + (a * 0.044715) * (v * v)))
            stage[rows, x] = v.astype(BF).reshape(share, ROWS, DEPTH)
        copies.append(pltpu.make_async_copy(stage.at[rows], out_ref.at[rows], sems.at[q]))
        copies[-1].start()
    for copy in copies:
        copy.wait()


def call(kernel, name, args, outs, scratch=(), spaces=None):
    spaces = spaces or [pltpu.VMEM] * len(args)
    args = [x if s is pl.ANY else pltpu.with_memory_space_constraint(x, s) for x, s in zip(args, spaces)]
    spec = lambda s: pl.BlockSpec(memory_space=pl.ANY if s is pltpu.HBM else s)
    return pl.pallas_call(
        kernel,
        out_shape=outs,
        in_specs=[spec(s) for s in spaces],
        out_specs=jax.tree.map(lambda o: spec(o.memory_space), outs),
        scratch_shapes=list(scratch),
        compiler_params=pltpu.CompilerParams(vmem_limit_bytes=12 * 2**20),
        name=name,
    )(*args)


def shards(field, spectral_weight, point_weight, bias):
    front, across, along, back, planes = (jnp.asarray(t) for t in tables())
    swap = [(0, 1), (1, 0)]
    vm = lambda *shape, dtype=BF: pltpu.VMEM(shape, dtype)
    dma = pltpu.SemaphoreType.DMA

    peer_weight = lax.ppermute(spectral_weight, "c", swap)
    own, send, back, planes, grid = call(
        analysis_kernel,
        "analysis",
        (field, front, across, back, planes),
        (vm(128, 512), vm(128, 512), vm(48, DEPTH), vm(128, 128), vm(C, X, ROWS, DEPTH)),
        (
            vm(X * DEPTH, 256),
            vm(DEPTH, 256),
            vm(X, 256, dtype=F32),
            dma,
            dma((4,)),
        ),
        (pltpu.HBM,) * 5,
    )
    recv = lax.ppermute(send, "c", swap)
    wy, kron, shift, spread = call(
        tables_kernel,
        "tables",
        (along, point_weight, bias.reshape(1, 32)),
        (vm(256, 256), vm(512, 512), vm(16, 512), vm(128, 512)),
        (vm(32, 32), dma),
        (pltpu.HBM, pltpu.VMEM, pltpu.VMEM),
    )
    parts = call(
        rows_kernel,
        "rows",
        (own, recv, wy, peer_weight),
        vm(1024, 128),
        (vm(1024, 128, dtype=F32),),
        (pltpu.VMEM, pltpu.VMEM, pltpu.VMEM, pl.ANY),
    )
    parts = lax.all_to_all(parts.reshape(128, 8, 128), ("x", "y", "z"), 0, 0, tiled=True)
    mixed = call(
        mix_kernel,
        "mix",
        (parts.reshape(1024, 128), spectral_weight, peer_weight, spread),
        vm(1024, 128),
    )
    modes = lax.all_to_all(mixed.reshape(128, 8, 128), ("x", "y", "z"), 0, 0, tiled=True)
    own, send = call(
        modes_kernel,
        "modes",
        (modes.reshape(1024, 128), wy, planes),
        (vm(128, 512), vm(128, 512)),
        (vm(1024, 128, dtype=F32),),
    )
    recv = lax.ppermute(send, "c", swap)
    point = call(
        point_kernel,
        "point",
        (grid, kron, own),
        vm(X, C * ROWS, DEPTH, dtype=F32),
        (),
        (pltpu.VMEM, pltpu.VMEM, pl.ANY),
    )
    return call(
        grid_kernel,
        "grid",
        (point, own, recv, shift, back),
        pltpu.HBM((C, X, ROWS, DEPTH), BF),
        (vm(C, X, ROWS, DEPTH), dma((CHUNKS,))),
    )


def solution(mesh):
    fine = Mesh(mesh.devices.reshape(DZ, DY, DC, DX), ("z", "y", "c", "x"))
    return jax.shard_map(
        shards,
        mesh=fine,
        in_specs=(P(None, None, ("z", "y", "c"), "x"), P(("z", "y", "c"), "x", None), P(), P()),
        out_specs=P(None, None, ("z", "y", "c"), "x"),
        check_vma=False,
    )
```

```python
import math

import jax
import jax.numpy as jnp
import ml_dtypes
import numpy as np
from jax import lax
from jax.experimental import pallas as pl
from jax.experimental.pallas import tpu as pltpu
from jax.sharding import Mesh
from jax.sharding import PartitionSpec as P

C, X, K, N = 32, 8, 32, 1024
DZ, DY, DC, DX = 8, 4, 2, 4
ROWS = N // (DZ * DY * DC)
DEPTH = N // DX
CHUNKS = 4
BF = jnp.bfloat16
F32 = jnp.float32


def cosines(count, length, norm):
    modes = np.arange(count, dtype=np.float64)[:, None]
    spots = np.arange(length, dtype=np.float64)[None, :]
    value = norm * np.cos(np.pi * modes * (spots + 0.5) / length)
    value[0] *= math.sqrt(0.5)
    return value


def tables():
    ax = cosines(X, X, math.sqrt(2.0 / X))
    ay = cosines(K, N, math.sqrt(2.0 / N))
    az = cosines(K, N, math.sqrt(2.0 / N)).astype(ml_dtypes.bfloat16).astype(np.float64)
    sz = cosines(K, N, math.sqrt(2.0 / K))
    kq, kx, i = np.meshgrid(np.arange(4), np.arange(DX), np.arange(X), indexing="ij")
    front = np.zeros((DX, DC, DEPTH, 2, 128))
    for core in range(DC):
        for h in range(2):
            k = (kx * 8 + (core ^ h) * 4 + kq).reshape(-1)
            front[:, core, :, h] = az[k].reshape(128, DX, DEPTH).transpose(1, 2, 0)
    across = np.tile(ax[i.reshape(-1)].T, (1, 2))
    along = np.zeros((DZ * DY * DC, 32, 32))
    for dev in range(DZ * DY * DC):
        core = dev % 2
        spots = np.concatenate([dev * ROWS + np.arange(ROWS), (dev ^ 1) * ROWS + np.arange(ROWS)])
        octet = np.concatenate([core * 4 + np.arange(4), (1 - core) * 4 + np.arange(4)])
        j = (np.arange(4)[:, None] * 8 + octet[None, :]).reshape(-1)
        along[dev] = ay[j][:, spots].T
    back = np.zeros((DX * DC, 48, DEPTH))
    q2, x2 = np.meshgrid(np.arange(4), np.arange(DX), indexing="ij")
    for chip in range(DX):
        for core in range(DC):
            own = (x2 * 8 + core * 4 + q2).reshape(-1)
            other = (x2 * 8 + (1 - core) * 4 + q2).reshape(-1)
            part = slice(chip * DEPTH, (chip + 1) * DEPTH)
            back[chip * 2 + core, :16] = sz[own][:, part]
            back[chip * 2 + core, 16:32] = sz[other][:, part]
            back[chip * 2 + core, 32:35] = 1.0
    planes = np.zeros((2, X, 4, DX, DX, X, 2, 4))
    for g in range(2):
        for q in range(4):
            for chip in range(DX):
                planes[g, :, q, chip, chip, :, g, q] = ax.T * math.sqrt(N / K)
    bf = ml_dtypes.bfloat16
    return (
        front.reshape(DX, DC, DEPTH, 256).astype(bf),
        across.astype(np.float32),
        along.astype(bf),
        back.astype(bf),
        planes.reshape(256, 256).astype(bf),
    )


def dot(a, b, dims=((1,), (0,))):
    return lax.dot_general(a, b, (dims, ((), ())), preferred_element_type=F32)


def iota(shape, dim):
    return lax.broadcasted_iota(jnp.int32, shape, dim)


def ones_where(condition):
    return jnp.where(condition, 1.0, 0.0).astype(BF)


def at_chip():
    return lax.axis_index("x")


def at_core():
    return lax.axis_index("c")


def at_rows():
    return (lax.axis_index("z") * DY + lax.axis_index("y")) * DC + lax.axis_index("c")


def analysis_kernel(
    field, front, across, back, planes, along, weight,
    own, send, back_out, planes_out, along_out, grid,
    weights, base, vectors, mixing, field_sem, sems,
):
    copy = pltpu.make_async_copy(field, grid, field_sem)
    loads = [
        pltpu.make_async_copy(source, target, sems.at[at])
        for at, (source, target) in enumerate(
            (
                (front.at[at_chip(), at_core()], base),
                (across, vectors),
                (weight, mixing),
                (back.at[at_chip() * DC + at_core()], back_out),
                (planes, planes_out),
                (along.at[at_rows()], along_out),
            )
        )
    ]
    loads[0].start()
    loads[1].start()
    copy.start()
    for load in loads[2:]:
        load.start()
    loads[0].wait()
    loads[1].wait()
    wide = base[...].astype(F32)
    for x in range(X):
        weights[pl.ds(x * DEPTH, DEPTH), :] = (wide * vectors[pl.ds(x, 1), :]).astype(BF)
    for load in loads[2:]:
        load.wait()
    given = mixing[...].reshape(32, 1024)
    send[128:160, :] = given[:, :512]
    send[160:192, :] = given[:, 512:]
    copy.wait()
    lhs = jnp.concatenate([grid[:, x].reshape(C * ROWS, DEPTH) for x in range(X)], axis=1)
    res = dot(lhs, weights[...]).T.astype(BF)
    own[...] = res[:128]
    send[:128, :] = res[128:]


def tables_kernel(along_ref, point_ref, bias_ref, wy, order_ref, kron_ref, shift_ref):
    to, source = iota((256, 256), 0), iota((256, 256), 1)
    order_ref[...] = ones_where(source == (to // 4 % 2) * 128 + (to % 4) * 32 + to // 8)
    e1 = ones_where(iota((512, 32), 0) // 16 == iota((512, 32), 1))
    e2 = ones_where(iota((32, 512), 0) == iota((32, 512), 1) // 16)
    wide = dot(dot(e1, point_ref[...], ((1,), (1,))).astype(BF), e2)
    same = iota((512, 512), 0) % 16 == iota((512, 512), 1) % 16
    kron_ref[...] = jnp.where(same, wide, 0.0).astype(BF)
    b = jnp.broadcast_to(bias_ref[...], (16, 32))
    b1 = b.astype(BF).astype(F32)
    b2 = (b - b1).astype(BF).astype(F32)
    b3 = b - b1 - b2
    row = iota((16, 32), 0)
    parts = jnp.where(row == 0, b1, jnp.where(row == 1, b2, jnp.where(row == 2, b3, 0.0)))
    shift_ref[...] = dot(parts.astype(BF), e2).astype(BF)
    p1 = ones_where(
        (iota((256, 32), 0) // 128 == iota((256, 32), 1) // 16)
        & (iota((256, 32), 0) % 16 == iota((256, 32), 1) % 16)
    )
    p2 = ones_where(
        (iota((32, 256), 0) // 8 == iota((32, 256), 1) // 64)
        & (iota((32, 256), 0) % 8 == iota((32, 256), 1) % 8)
    )
    same = (iota((256, 256), 0) // 16) % 8 == (iota((256, 256), 1) // 8) % 8
    full = dot(dot(p1, along_ref[...]).astype(BF), p2)
    wy[...] = jnp.where(same, full, 0.0).astype(BF)


def rows_kernel(own_ref, recv_ref, wy_ref, order_ref, out_ref, peer_out):
    blocks = []
    for e in range(2):
        halves = []
        for g in range(2):
            part = pl.ds((g * 2 + e) * 128, 128)
            halves.append(dot(jnp.concatenate([own_ref[:, part], recv_ref[:128, part]], axis=1), wy_ref[...]))
        blocks.append(dot(order_ref[...], jnp.concatenate(halves, axis=0).astype(BF)))
    for joct in range(4):
        cols = slice(joct * 64, (joct + 1) * 64)
        res = jnp.concatenate([blocks[0][:, cols], blocks[1][:, cols]], axis=1)
        for to in range(32):
            out_ref[pl.ds((to * 4 + joct) * 8, 8), :] = res[to * 8 : (to + 1) * 8, :].astype(BF)
    peer_out[...] = recv_ref[128:192, :]


def mix_kernel(parts_ref, weight_ref, peer_ref, out_ref):
    core = at_core()
    s = jnp.sum(parts_ref[...].astype(F32).reshape(128, 8, 128), axis=0)
    row = iota((8, 128), 0)
    turned = pltpu.roll(s, 4, 0)
    s8 = jnp.concatenate([jnp.where(row < 4, s, turned), jnp.where(row < 4, turned, s)], axis=1)
    s64 = jnp.concatenate([s8] * 8, axis=0)
    row = iota((64, 256), 0)
    keep = (iota((64, 256), 1) % 8 == row // 8) & ((row % 8) // 4 == core)
    s64 = jnp.where(keep, s64, 0.0)
    high = s64.astype(BF)
    low = (s64 - high.astype(F32)).astype(BF)
    spread = ones_where(iota((128, 512), 0) // 8 == iota((128, 512), 1) // 32)
    halves = [dot(high[:, part], spread) + dot(low[:, part], spread) for part in (slice(0, 128), slice(128, 256))]
    wide = jnp.concatenate(halves, axis=1)
    peer = jnp.concatenate([peer_ref[:32, :], peer_ref[32:, :]], axis=1)
    weight = jnp.concatenate([weight_ref[...].reshape(32, 1024), peer], axis=0).astype(F32)
    prod = wide * weight
    total = prod[:, 0:128]
    for part in range(1, 8):
        total = total + prod[:, part * 128 : (part + 1) * 128]
    total = total + pltpu.roll(total, 64, 1)
    total = total + pltpu.roll(total, 32, 1)
    mixed = total.astype(BF)
    q, col = iota((128, 256), 0), iota((128, 256), 1)
    place = ones_where(q == (col // 128) * 16 + (col % 128) // 8)
    placed = dot(mixed, place)
    placed = jnp.where(iota((64, 256), 1) % 8 == iota((64, 256), 0) // 8, placed, 0.0).astype(BF)
    take = ones_where(iota((8, 64), 0) % 4 == iota((8, 64), 1) % 4)
    both = dot(take, placed)
    out = jnp.where(iota((8, 128), 0) < 4, both[:, :128], both[:, 128:])
    out_ref[...] = jnp.broadcast_to(out[None], (128, 8, 128)).reshape(1024, 128).astype(BF)


def modes_kernel(modes_ref, wy_ref, planes_ref, own_ref, send_ref):
    for e in range(2):
        lanes = slice(e * 64, (e + 1) * 64)
        rows = []
        for kx in range(4):
            for i in range(8):
                at = ((kx * 8 + i) * 4) * 8
                cols = [modes_ref[pl.ds(at + joct * 8, 8), :][:, lanes] for joct in range(4)]
                rows.append(jnp.concatenate(cols, axis=1))
        res = dot(jnp.concatenate(rows, axis=0), wy_ref[...], ((1,), (1,))).astype(BF)
        res = dot(planes_ref[...], res).astype(BF)
        for g in range(2):
            part = pl.ds((g * 2 + e) * 128, 128)
            own_ref[:, part] = res[g * 128 : (g + 1) * 128, :128]
            send_ref[:, part] = res[g * 128 : (g + 1) * 128, 128:]


def point_kernel(grid_ref, kron_ref, after_ref, out_ref):
    for x in range(X):
        out_ref[x] = dot(kron_ref[...], grid_ref[:, x].reshape(C * ROWS, DEPTH))


def grid_kernel(point_ref, own_ref, recv_ref, shift_ref, back_ref, out_ref, stage, sems):
    a = 2.0 * math.sqrt(2.0 / math.pi)
    share = C // CHUNKS
    copies = []
    for q in range(CHUNKS):
        cols = pl.ds(q * share * ROWS, share * ROWS)
        rows = pl.ds(q * share, share)
        for x in range(X):
            part = pl.ds(x * 16, 16)
            modes = jnp.concatenate([own_ref[part, cols], recv_ref[part, cols], shift_ref[:, cols]], axis=0)
            v = point_ref[x, cols, :] + dot(modes, back_ref[...], ((0,), (0,)))
            v = v * jax.nn.sigmoid(v * (a + (a * 0.044715) * (v * v)))
            stage[rows, x] = v.astype(BF).reshape(share, ROWS, DEPTH)
        copies.append(pltpu.make_async_copy(stage.at[rows], out_ref.at[rows], sems.at[q]))
        copies[-1].start()
    for copy in copies:
        copy.wait()


def call(kernel, name, args, outs, scratch=(), spaces=None):
    spaces = spaces or [pltpu.VMEM] * len(args)
    args = [x if s is pl.ANY else pltpu.with_memory_space_constraint(x, s) for x, s in zip(args, spaces)]
    spec = lambda s: pl.BlockSpec(memory_space=pl.ANY if s is pltpu.HBM else s)
    return pl.pallas_call(
        kernel,
        out_shape=outs,
        in_specs=[spec(s) for s in spaces],
        out_specs=jax.tree.map(lambda o: spec(o.memory_space), outs),
        scratch_shapes=list(scratch),
        compiler_params=pltpu.CompilerParams(vmem_limit_bytes=12 * 2**20),
        name=name,
    )(*args)


def shards(field, spectral_weight, point_weight, bias):
    front, across, along, back, planes = (jnp.asarray(t) for t in tables())
    swap = [(0, 1), (1, 0)]
    vm = lambda *shape, dtype=BF: pltpu.VMEM(shape, dtype)
    dma = pltpu.SemaphoreType.DMA

    own, send, back, planes, along, grid = call(
        analysis_kernel,
        "analysis",
        (field, front, across, back, planes, along, spectral_weight),
        (vm(128, 512), vm(192, 512), vm(48, DEPTH), vm(256, 256), vm(32, 32), vm(C, X, ROWS, DEPTH)),
        (
            vm(X * DEPTH, 256),
            vm(DEPTH, 256),
            vm(X, 256, dtype=F32),
            vm(4, 8, 1024),
            dma,
            dma((6,)),
        ),
        (pltpu.HBM,) * 7,
    )
    recv = lax.ppermute(send, "c", swap)
    wy, order, kron, shift = call(
        tables_kernel,
        "tables",
        (along, point_weight, bias.reshape(1, 32)),
        (vm(256, 256), vm(256, 256), vm(512, 512), vm(16, 512)),
    )
    parts, peer_weight = call(
        rows_kernel,
        "rows",
        (own, recv, wy, order),
        (vm(1024, 128), vm(64, 512)),
    )
    parts = lax.all_to_all(parts.reshape(128, 8, 128), ("x", "z", "y"), 0, 0, tiled=True)
    mixed = call(
        mix_kernel,
        "mix",
        (parts.reshape(1024, 128), spectral_weight, peer_weight),
        vm(1024, 128),
    )
    modes = lax.all_to_all(mixed.reshape(128, 8, 128), ("x", "z", "y"), 0, 0, tiled=True)
    own, send = call(
        modes_kernel,
        "modes",
        (modes.reshape(1024, 128), wy, planes),
        (vm(128, 512), vm(128, 512)),
    )
    recv = lax.ppermute(send, "c", swap)
    point = call(
        point_kernel,
        "point",
        (grid, kron, own),
        vm(X, C * ROWS, DEPTH, dtype=F32),
        (),
        (pltpu.VMEM, pltpu.VMEM, pl.ANY),
    )
    return call(
        grid_kernel,
        "grid",
        (point, own, recv, shift, back),
        pltpu.HBM((C, X, ROWS, DEPTH), BF),
        (vm(C, X, ROWS, DEPTH), dma((CHUNKS,))),
    )


def solution(mesh):
    fine = Mesh(mesh.devices.reshape(DZ, DY, DC, DX), ("z", "y", "c", "x"))
    return jax.shard_map(
        shards,
        mesh=fine,
        in_specs=(P(None, None, ("z", "y", "c"), "x"), P(("z", "y", "c"), "x", None), P(), P()),
        out_specs=P(None, None, ("z", "y", "c"), "x"),
        check_vma=False,
    )
```

```python
import math

import jax
import jax.numpy as jnp
import ml_dtypes
import numpy as np
from jax import lax
from jax.experimental import pallas as pl
from jax.experimental.pallas import tpu as pltpu
from jax.sharding import Mesh
from jax.sharding import PartitionSpec as P

C, X, K, N = 32, 8, 32, 1024
DZ, DY, DC, DX = 8, 4, 2, 4
ROWS = N // (DZ * DY * DC)
DEPTH = N // DX
CHUNKS = 4
BF = jnp.bfloat16
F32 = jnp.float32


def cosines(count, length, norm):
    modes = np.arange(count, dtype=np.float64)[:, None]
    spots = np.arange(length, dtype=np.float64)[None, :]
    value = norm * np.cos(np.pi * modes * (spots + 0.5) / length)
    value[0] *= math.sqrt(0.5)
    return value


def tables():
    ax = cosines(X, X, math.sqrt(2.0 / X))
    ay = cosines(K, N, math.sqrt(2.0 / N))
    az = cosines(K, N, math.sqrt(2.0 / N)).astype(ml_dtypes.bfloat16).astype(np.float64)
    sz = cosines(K, N, math.sqrt(2.0 / K))
    kq, kx, i = np.meshgrid(np.arange(4), np.arange(DX), np.arange(X), indexing="ij")
    front = np.zeros((DX, DC, DEPTH, 2, 128))
    for core in range(DC):
        for h in range(2):
            k = (kx * 8 + (core ^ h) * 4 + kq).reshape(-1)
            front[:, core, :, h] = az[k].reshape(128, DX, DEPTH).transpose(1, 2, 0)
    across = np.tile(ax[i.reshape(-1)].T, (1, 2))
    along = np.zeros((DZ * DY * DC, 32, 32))
    for dev in range(DZ * DY * DC):
        core = dev % 2
        spots = np.concatenate([dev * ROWS + np.arange(ROWS), (dev ^ 1) * ROWS + np.arange(ROWS)])
        octet = np.concatenate([core * 4 + np.arange(4), (1 - core) * 4 + np.arange(4)])
        j = (np.arange(4)[:, None] * 8 + octet[None, :]).reshape(-1)
        along[dev] = ay[j][:, spots].T
    back = np.zeros((DX * DC, 48, DEPTH))
    q2, x2 = np.meshgrid(np.arange(4), np.arange(DX), indexing="ij")
    for chip in range(DX):
        for core in range(DC):
            own = (x2 * 8 + core * 4 + q2).reshape(-1)
            other = (x2 * 8 + (1 - core) * 4 + q2).reshape(-1)
            part = slice(chip * DEPTH, (chip + 1) * DEPTH)
            back[chip * 2 + core, :16] = sz[own][:, part]
            back[chip * 2 + core, 16:32] = sz[other][:, part]
            back[chip * 2 + core, 32:35] = 1.0
    planes = np.zeros((2, X, 4, DX, DX, X, 2, 4))
    for g in range(2):
        for q in range(4):
            for chip in range(DX):
                planes[g, :, q, chip, chip, :, g, q] = ax.T * math.sqrt(N / K)
    bf = ml_dtypes.bfloat16
    return (
        front.reshape(DX, DC, DEPTH, 256).astype(bf),
        across.astype(np.float32),
        along.astype(bf),
        back.astype(bf),
        planes.reshape(256, 256).astype(bf),
    )


def dot(a, b, dims=((1,), (0,))):
    return lax.dot_general(a, b, (dims, ((), ())), preferred_element_type=F32)


def iota(shape, dim):
    return lax.broadcasted_iota(jnp.int32, shape, dim)


def ones_where(condition):
    return jnp.where(condition, 1.0, 0.0).astype(BF)


def at_chip():
    return lax.axis_index("x")


def at_core():
    return lax.axis_index("c")


def at_rows():
    return (lax.axis_index("z") * DY + lax.axis_index("y")) * DC + lax.axis_index("c")


def analysis_kernel(
    field, front, across, back, planes, along, weight,
    own, send, back_out, planes_out, along_out, grid,
    weights, base, vectors, mixing, field_sem, sems,
):
    copy = pltpu.make_async_copy(field, grid, field_sem)
    loads = [
        pltpu.make_async_copy(source, target, sems.at[at])
        for at, (source, target) in enumerate(
            (
                (front.at[at_chip(), at_core()], base),
                (across, vectors),
                (weight, mixing),
                (back.at[at_chip() * DC + at_core()], back_out),
                (planes, planes_out),
                (along.at[at_rows()], along_out),
            )
        )
    ]
    loads[0].start()
    loads[1].start()
    copy.start()
    for load in loads[2:]:
        load.start()
    loads[0].wait()
    loads[1].wait()
    wide = base[...].astype(F32)
    for x in range(X):
        weights[pl.ds(x * DEPTH, DEPTH), :] = (wide * vectors[pl.ds(x, 1), :]).astype(BF)
    for load in loads[2:]:
        load.wait()
    given = mixing[...].reshape(32, 1024)
    send[128:160, :] = given[:, :512]
    send[160:192, :] = given[:, 512:]
    copy.wait()
    lhs = jnp.concatenate([grid[:, x].reshape(C * ROWS, DEPTH) for x in range(X)], axis=1)
    res = dot(lhs, weights[...]).T.astype(BF)
    own[...] = res[:128]
    send[:128, :] = res[128:]


def tables_kernel(along_ref, point_ref, bias_ref, wy, order_ref, kron_ref, shift_ref):
    to, source = iota((256, 256), 0), iota((256, 256), 1)
    order_ref[...] = ones_where(source == (to // 4 % 2) * 128 + (to % 4) * 32 + to // 8)
    e1 = ones_where(iota((256, 32), 0) // 8 == iota((256, 32), 1))
    e2 = ones_where(iota((32, 256), 0) == iota((32, 256), 1) // 8)
    wide = dot(dot(e1, point_ref[...], ((1,), (1,))).astype(BF), e2)
    same = iota((256, 256), 0) % 8 == iota((256, 256), 1) % 8
    kron_ref[...] = jnp.where(same, wide, 0.0).astype(BF)
    b = jnp.broadcast_to(bias_ref[...], (16, 32))
    b1 = b.astype(BF).astype(F32)
    b2 = (b - b1).astype(BF).astype(F32)
    b3 = b - b1 - b2
    row = iota((16, 32), 0)
    parts = jnp.where(row == 0, b1, jnp.where(row == 1, b2, jnp.where(row == 2, b3, 0.0)))
    e3 = ones_where(iota((32, 512), 0) == iota((32, 512), 1) // 16)
    shift_ref[...] = dot(parts.astype(BF), e3).astype(BF)
    p1 = ones_where(
        (iota((512, 32), 0) // 256 == iota((512, 32), 1) // 16)
        & (iota((512, 32), 0) % 16 == iota((512, 32), 1) % 16)
    )
    p2 = ones_where(
        (iota((32, 512), 0) // 8 == iota((32, 512), 1) // 128)
        & (iota((32, 512), 0) % 8 == iota((32, 512), 1) % 8)
    )
    same = (iota((512, 512), 0) // 16) % 16 == (iota((512, 512), 1) // 8) % 16
    full = dot(dot(p1, along_ref[...]).astype(BF), p2)
    wy[...] = jnp.where(same, full, 0.0).astype(BF)


def rows_kernel(own_ref, recv_ref, wy_ref, order_ref, out_ref, peer_out):
    halves = []
    for g in range(2):
        part = pl.ds(g * 256, 256)
        halves.append(jnp.concatenate([own_ref[:, part], recv_ref[:128, part]], axis=1))
    lhs = dot(order_ref[...], jnp.concatenate(halves, axis=0)).astype(BF)
    res = dot(lhs, wy_ref[...])
    for to in range(32):
        for joct in range(4):
            out_ref[pl.ds((to * 4 + joct) * 8, 8), :] = res[
                to * 8 : (to + 1) * 8, joct * 128 : (joct + 1) * 128
            ].astype(BF)
    peer_out[...] = recv_ref[128:192, :]


def mix_kernel(parts_ref, weight_ref, peer_ref, out_ref):
    core = at_core()
    s = jnp.sum(parts_ref[...].astype(F32).reshape(128, 8, 128), axis=0)
    row = iota((8, 128), 0)
    turned = pltpu.roll(s, 4, 0)
    s8 = jnp.concatenate([jnp.where(row < 4, s, turned), jnp.where(row < 4, turned, s)], axis=1)
    s64 = jnp.concatenate([s8] * 8, axis=0)
    row = iota((64, 256), 0)
    keep = (iota((64, 256), 1) % 8 == row // 8) & ((row % 8) // 4 == core)
    s64 = jnp.where(keep, s64, 0.0)
    high = s64.astype(BF)
    low = (s64 - high.astype(F32)).astype(BF)
    parts = jnp.concatenate([high, low], axis=0)
    spread = ones_where(iota((128, 512), 0) // 8 == iota((128, 512), 1) // 32)
    peer = jnp.concatenate([peer_ref[:32, :], peer_ref[32:, :]], axis=1)
    weight = jnp.concatenate([weight_ref[...].reshape(32, 1024), peer], axis=0).astype(F32)
    total = jnp.zeros((64, 128), F32)
    for g in range(2):
        wide = dot(parts[:, g * 128 : (g + 1) * 128], spread)
        prod = (wide[:64] + wide[64:]) * weight[:, g * 512 : (g + 1) * 512]
        for part in range(4):
            total = total + prod[:, part * 128 : (part + 1) * 128]
    total = total + pltpu.roll(total, 64, 1)
    total = total + pltpu.roll(total, 32, 1)
    mixed = total.astype(BF)
    q, col = iota((128, 256), 0), iota((128, 256), 1)
    place = ones_where(q == (col // 128) * 16 + (col % 128) // 8)
    placed = dot(mixed, place)
    placed = jnp.where(iota((64, 256), 1) % 8 == iota((64, 256), 0) // 8, placed, 0.0)
    both = placed[:8]
    for j in range(1, 8):
        both = both + placed[j * 8 : (j + 1) * 8]
    both = both + pltpu.roll(both, 4, 0)
    out = jnp.where(iota((8, 128), 0) < 4, both[:, :128], both[:, 128:]).astype(BF)
    out_ref[...] = jnp.broadcast_to(out[None], (128, 8, 128)).reshape(1024, 128)


def modes_kernel(modes_ref, wy_ref, planes_ref, own_ref, send_ref):
    rows = []
    for to in range(32):
        cols = [modes_ref[pl.ds((to * 4 + joct) * 8, 8), :] for joct in range(4)]
        rows.append(jnp.concatenate(cols, axis=1))
    res = dot(jnp.concatenate(rows, axis=0), wy_ref[...], ((1,), (1,))).astype(BF)
    res = dot(planes_ref[...], res).astype(BF)
    for g in range(2):
        part = pl.ds(g * 256, 256)
        own_ref[:, part] = res[g * 128 : (g + 1) * 128, :256]
        send_ref[:, part] = res[g * 128 : (g + 1) * 128, 256:]


def point_kernel(grid_ref, kron_ref, after_ref, out_ref):
    for x in range(X):
        for half in range(2):
            part = slice(half * 8, half * 8 + 8)
            res = dot(kron_ref[...], grid_ref[:, x, part, :].reshape(C * 8, DEPTH))
            out_ref[x, :, part, :] = res.reshape(C, 8, DEPTH)


def grid_kernel(point_ref, own_ref, recv_ref, shift_ref, back_ref, out_ref, stage, sems):
    a = 2.0 * math.sqrt(2.0 / math.pi)
    share = C // CHUNKS
    copies = []
    for q in range(CHUNKS):
        cols = pl.ds(q * share * ROWS, share * ROWS)
        rows = pl.ds(q * share, share)
        for x in range(X):
            part = pl.ds(x * 16, 16)
            modes = jnp.concatenate([own_ref[part, cols], recv_ref[part, cols], shift_ref[:, cols]], axis=0)
            v = point_ref[x, rows].reshape(share * ROWS, DEPTH) + dot(modes, back_ref[...], ((0,), (0,)))
            v = v.astype(BF)
            v = v * jax.nn.sigmoid(v * (jnp.asarray(a, BF) + jnp.asarray(a * 0.044715, BF) * (v * v)))
            stage[rows, x] = v.reshape(share, ROWS, DEPTH)
        copies.append(pltpu.make_async_copy(stage.at[rows], out_ref.at[rows], sems.at[q]))
        copies[-1].start()
    for copy in copies:
        copy.wait()


def call(kernel, name, args, outs, scratch=(), spaces=None):
    spaces = spaces or [pltpu.VMEM] * len(args)
    args = [x if s is pl.ANY else pltpu.with_memory_space_constraint(x, s) for x, s in zip(args, spaces)]
    spec = lambda s: pl.BlockSpec(memory_space=pl.ANY if s is pltpu.HBM else s)
    return pl.pallas_call(
        kernel,
        out_shape=outs,
        in_specs=[spec(s) for s in spaces],
        out_specs=jax.tree.map(lambda o: spec(o.memory_space), outs),
        scratch_shapes=list(scratch),
        compiler_params=pltpu.CompilerParams(vmem_limit_bytes=12 * 2**20),
        name=name,
    )(*args)


def shards(field, spectral_weight, point_weight, bias):
    front, across, along, back, planes = (jnp.asarray(t) for t in tables())
    swap = [(0, 1), (1, 0)]
    vm = lambda *shape, dtype=BF: pltpu.VMEM(shape, dtype)
    dma = pltpu.SemaphoreType.DMA

    own, send, back, planes, along, grid = call(
        analysis_kernel,
        "analysis",
        (field, front, across, back, planes, along, spectral_weight),
        (vm(128, 512), vm(192, 512), vm(48, DEPTH), vm(256, 256), vm(32, 32), vm(C, X, ROWS, DEPTH)),
        (
            vm(X * DEPTH, 256),
            vm(DEPTH, 256),
            vm(X, 256, dtype=F32),
            vm(4, 8, 1024),
            dma,
            dma((6,)),
        ),
        (pltpu.HBM,) * 7,
    )
    recv = lax.ppermute(send, "c", swap)
    wy, order, kron, shift = call(
        tables_kernel,
        "tables",
        (along, point_weight, bias.reshape(1, 32)),
        (vm(512, 512), vm(256, 256), vm(256, 256), vm(16, 512)),
    )
    parts, peer_weight = call(
        rows_kernel,
        "rows",
        (own, recv, wy, order),
        (vm(1024, 128), vm(64, 512)),
    )
    parts = lax.all_to_all(parts.reshape(128, 8, 128), ("x", "z", "y"), 0, 0, tiled=True)
    mixed = call(
        mix_kernel,
        "mix",
        (parts.reshape(1024, 128), spectral_weight, peer_weight),
        vm(1024, 128),
    )
    modes = lax.all_to_all(mixed.reshape(128, 8, 128), ("x", "z", "y"), 0, 0, tiled=True)
    own, send = call(
        modes_kernel,
        "modes",
        (modes.reshape(1024, 128), wy, planes),
        (vm(128, 512), vm(128, 512)),
    )
    recv = lax.ppermute(send, "c", swap)
    point = call(
        point_kernel,
        "point",
        (grid, kron, own),
        vm(X, C, ROWS, DEPTH, dtype=F32),
        (),
        (pltpu.VMEM, pltpu.VMEM, pl.ANY),
    )
    return call(
        grid_kernel,
        "grid",
        (point, own, recv, shift, back),
        pltpu.HBM((C, X, ROWS, DEPTH), BF),
        (vm(C, X, ROWS, DEPTH), dma((CHUNKS,))),
    )


def solution(mesh):
    fine = Mesh(mesh.devices.reshape(DZ, DY, DC, DX), ("z", "y", "c", "x"))
    return jax.shard_map(
        shards,
        mesh=fine,
        in_specs=(P(None, None, ("z", "y", "c"), "x"), P(("z", "y", "c"), "x", None), P(), P()),
        out_specs=P(None, None, ("z", "y", "c"), "x"),
        check_vma=False,
    )
```

```python
import math

import jax
import jax.numpy as jnp
import ml_dtypes
import numpy as np
from jax import lax
from jax.experimental import pallas as pl
from jax.experimental.pallas import tpu as pltpu
from jax.sharding import Mesh
from jax.sharding import PartitionSpec as P

C, X, K, N = 32, 8, 32, 1024
DZ, DY, DC, DX = 8, 4, 2, 4
ROWS = N // (DZ * DY * DC)
DEPTH = N // DX
CHUNKS = 4
BF = jnp.bfloat16
F32 = jnp.float32


CHIPS = [(x, z, y) for x in range(DX) for z in range(DZ) for y in range(DY)]
ORDER = sorted(CHIPS, key=lambda chip: chip != (2, 5, 2))
SLOT = {chip: at for at, chip in enumerate(ORDER)}
GROUP = [[CHIPS.index(chip) for chip in ORDER]]


def cosines(count, length, norm):
    modes = np.arange(count, dtype=np.float64)[:, None]
    spots = np.arange(length, dtype=np.float64)[None, :]
    value = norm * np.cos(np.pi * modes * (spots + 0.5) / length)
    value[0] *= math.sqrt(0.5)
    return value


def tables():
    ax = cosines(X, X, math.sqrt(2.0 / X))
    ay = cosines(K, N, math.sqrt(2.0 / N))
    az = cosines(K, N, math.sqrt(2.0 / N)).astype(ml_dtypes.bfloat16).astype(np.float64)
    sz = cosines(K, N, math.sqrt(2.0 / K))
    kq, kx, i = np.meshgrid(np.arange(4), np.arange(DX), np.arange(X), indexing="ij")
    front = np.zeros((DX, DC, DEPTH, 2, 128))
    for core in range(DC):
        for h in range(2):
            k = (kx * 8 + (core ^ h) * 4 + kq).reshape(-1)
            front[:, core, :, h] = az[k].reshape(128, DX, DEPTH).transpose(1, 2, 0)
    across = np.tile(ax[i.reshape(-1)].T, (1, 2))
    along = np.zeros((DZ * DY * DC, 32, 32))
    for dev in range(DZ * DY * DC):
        core = dev % 2
        spots = np.concatenate([dev * ROWS + np.arange(ROWS), (dev ^ 1) * ROWS + np.arange(ROWS)])
        octet = np.concatenate([core * 4 + np.arange(4), (1 - core) * 4 + np.arange(4)])
        j = (np.arange(4)[:, None] * 8 + octet[None, :]).reshape(-1)
        along[dev] = ay[j][:, spots].T
    back = np.zeros((DX * DC, 48, DEPTH))
    q2, x2 = np.meshgrid(np.arange(4), np.arange(DX), indexing="ij")
    for chip in range(DX):
        for core in range(DC):
            own = (x2 * 8 + core * 4 + q2).reshape(-1)
            other = (x2 * 8 + (1 - core) * 4 + q2).reshape(-1)
            part = slice(chip * DEPTH, (chip + 1) * DEPTH)
            back[chip * 2 + core, :16] = sz[own][:, part]
            back[chip * 2 + core, 16:32] = sz[other][:, part]
            back[chip * 2 + core, 32:35] = 1.0
    planes = np.zeros((2, X, 4, DX, DX, X, 2, 4))
    for g in range(2):
        for q in range(4):
            for chip in range(DX):
                planes[g, :, q, chip, chip, :, g, q] = ax.T * math.sqrt(N / K)
    bf = ml_dtypes.bfloat16
    return (
        front.reshape(DX, DC, DEPTH, 256).astype(bf),
        across.astype(np.float32),
        along.astype(bf),
        back.astype(bf),
        planes.reshape(256, 256).astype(bf),
    )


def dot(a, b, dims=((1,), (0,))):
    return lax.dot_general(a, b, (dims, ((), ())), preferred_element_type=F32)


def iota(shape, dim):
    return lax.broadcasted_iota(jnp.int32, shape, dim)


def ones_where(condition):
    return jnp.where(condition, 1.0, 0.0).astype(BF)


def at_chip():
    return lax.axis_index("x")


def at_core():
    return lax.axis_index("c")


def at_rows():
    return (lax.axis_index("z") * DY + lax.axis_index("y")) * DC + lax.axis_index("c")


def analysis_kernel(
    field, front, across, back, planes, along, weight,
    own, send, back_out, planes_out, along_out, grid,
    weights, base, vectors, mixing, field_sem, sems,
):
    copy = pltpu.make_async_copy(field, grid, field_sem)
    loads = [
        pltpu.make_async_copy(source, target, sems.at[at])
        for at, (source, target) in enumerate(
            (
                (front.at[at_chip(), at_core()], base),
                (across, vectors),
                (weight, mixing),
                (back.at[at_chip() * DC + at_core()], back_out),
                (planes, planes_out),
                (along.at[at_rows()], along_out),
            )
        )
    ]
    loads[0].start()
    loads[1].start()
    copy.start()
    for load in loads[2:]:
        load.start()
    loads[0].wait()
    loads[1].wait()
    wide = base[...].astype(F32)
    for x in range(X):
        weights[pl.ds(x * DEPTH, DEPTH), :] = (wide * vectors[pl.ds(x, 1), :]).astype(BF)
    for load in loads[2:]:
        load.wait()
    given = mixing[...].reshape(32, 1024)
    send[128:160, :] = given[:, :512]
    send[160:192, :] = given[:, 512:]
    copy.wait()
    lhs = jnp.concatenate([grid[:, x].reshape(C * ROWS, DEPTH) for x in range(X)], axis=1)
    res = dot(lhs, weights[...]).T.astype(BF)
    own[...] = res[:128]
    send[:128, :] = res[128:]


def tables_kernel(along_ref, point_ref, bias_ref, wy, order_ref, kron_ref, shift_ref):
    to, source = iota((256, 256), 0), iota((256, 256), 1)
    order_ref[...] = ones_where(source == (to // 4 % 2) * 128 + (to % 4) * 32 + to // 8)
    e1 = ones_where(iota((256, 32), 0) // 8 == iota((256, 32), 1))
    e2 = ones_where(iota((32, 256), 0) == iota((32, 256), 1) // 8)
    wide = dot(dot(e1, point_ref[...], ((1,), (1,))).astype(BF), e2)
    same = iota((256, 256), 0) % 8 == iota((256, 256), 1) % 8
    kron_ref[...] = jnp.where(same, wide, 0.0).astype(BF)
    b = jnp.broadcast_to(bias_ref[...], (16, 32))
    b1 = b.astype(BF).astype(F32)
    b2 = (b - b1).astype(BF).astype(F32)
    b3 = b - b1 - b2
    row = iota((16, 32), 0)
    parts = jnp.where(row == 0, b1, jnp.where(row == 1, b2, jnp.where(row == 2, b3, 0.0)))
    e3 = ones_where(iota((32, 512), 0) == iota((32, 512), 1) // 16)
    shift_ref[...] = dot(parts.astype(BF), e3).astype(BF)
    p1 = ones_where(
        (iota((512, 32), 0) // 256 == iota((512, 32), 1) // 16)
        & (iota((512, 32), 0) % 16 == iota((512, 32), 1) % 16)
    )
    p2 = ones_where(
        (iota((32, 512), 0) // 8 == iota((32, 512), 1) // 128)
        & (iota((32, 512), 0) % 8 == iota((32, 512), 1) % 8)
    )
    same = (iota((512, 512), 0) // 16) % 16 == (iota((512, 512), 1) // 8) % 16
    full = dot(dot(p1, along_ref[...]).astype(BF), p2)
    wy[...] = jnp.where(same, full, 0.0).astype(BF)


def rows_kernel(own_ref, recv_ref, wy_ref, order_ref, out_ref, peer_out):
    halves = []
    for g in range(2):
        part = pl.ds(g * 256, 256)
        halves.append(jnp.concatenate([own_ref[:, part], recv_ref[:128, part]], axis=1))
    lhs = dot(order_ref[...], jnp.concatenate(halves, axis=0)).astype(BF)
    res = dot(lhs, wy_ref[...])
    for to in range(32):
        for joct in range(4):
            out_ref[pl.ds(SLOT[to // 8, to % 8, joct] * 8, 8), :] = res[
                to * 8 : (to + 1) * 8, joct * 128 : (joct + 1) * 128
            ].astype(BF)
    peer_out[...] = recv_ref[128:192, :]


def mix_kernel(parts_ref, weight_ref, peer_ref, out_ref):
    core = at_core()
    s = jnp.sum(parts_ref[...].astype(F32).reshape(128, 8, 128), axis=0)
    row = iota((8, 128), 0)
    turned = pltpu.roll(s, 4, 0)
    s8 = jnp.concatenate([jnp.where(row < 4, s, turned), jnp.where(row < 4, turned, s)], axis=1)
    s64 = jnp.concatenate([s8] * 8, axis=0)
    row = iota((64, 256), 0)
    keep = (iota((64, 256), 1) % 8 == row // 8) & ((row % 8) // 4 == core)
    s64 = jnp.where(keep, s64, 0.0)
    high = s64.astype(BF)
    low = (s64 - high.astype(F32)).astype(BF)
    parts = jnp.concatenate([high, low], axis=0)
    spread = ones_where(iota((128, 512), 0) // 8 == iota((128, 512), 1) // 32)
    peer = jnp.concatenate([peer_ref[:32, :], peer_ref[32:, :]], axis=1)
    weight = jnp.concatenate([weight_ref[...].reshape(32, 1024), peer], axis=0).astype(F32)
    total = jnp.zeros((64, 128), F32)
    for g in range(2):
        wide = dot(parts[:, g * 128 : (g + 1) * 128], spread)
        prod = (wide[:64] + wide[64:]) * weight[:, g * 512 : (g + 1) * 512]
        for part in range(4):
            total = total + prod[:, part * 128 : (part + 1) * 128]
    total = total + pltpu.roll(total, 64, 1)
    total = total + pltpu.roll(total, 32, 1)
    mixed = total.astype(BF)
    q, col = iota((128, 256), 0), iota((128, 256), 1)
    place = ones_where(q == (col // 128) * 16 + (col % 128) // 8)
    placed = dot(mixed, place)
    placed = jnp.where(iota((64, 256), 1) % 8 == iota((64, 256), 0) // 8, placed, 0.0)
    both = placed[:8]
    for j in range(1, 8):
        both = both + placed[j * 8 : (j + 1) * 8]
    both = both + pltpu.roll(both, 4, 0)
    out = jnp.where(iota((8, 128), 0) < 4, both[:, :128], both[:, 128:]).astype(BF)
    out_ref[...] = jnp.broadcast_to(out[None], (128, 8, 128)).reshape(1024, 128)


def modes_kernel(modes_ref, wy_ref, planes_ref, own_ref, send_ref):
    rows = []
    for to in range(32):
        cols = [modes_ref[pl.ds(SLOT[to // 8, to % 8, joct] * 8, 8), :] for joct in range(4)]
        rows.append(jnp.concatenate(cols, axis=1))
    res = dot(jnp.concatenate(rows, axis=0), wy_ref[...], ((1,), (1,))).astype(BF)
    res = dot(planes_ref[...], res).astype(BF)
    for g in range(2):
        part = pl.ds(g * 256, 256)
        own_ref[:, part] = res[g * 128 : (g + 1) * 128, :256]
        send_ref[:, part] = res[g * 128 : (g + 1) * 128, 256:]


def point_kernel(grid_ref, kron_ref, after_ref, out_ref):
    for x in range(X):
        for half in range(2):
            part = slice(half * 8, half * 8 + 8)
            res = dot(kron_ref[...], grid_ref[:, x, part, :].reshape(C * 8, DEPTH))
            out_ref[x, :, part, :] = res.reshape(C, 8, DEPTH)


def grid_kernel(point_ref, own_ref, recv_ref, shift_ref, back_ref, out_ref, stage, sems):
    a = 2.0 * math.sqrt(2.0 / math.pi)
    share = C // CHUNKS
    copies = []
    for q in range(CHUNKS):
        cols = pl.ds(q * share * ROWS, share * ROWS)
        rows = pl.ds(q * share, share)
        for x in range(X):
            part = pl.ds(x * 16, 16)
            modes = jnp.concatenate([own_ref[part, cols], recv_ref[part, cols], shift_ref[:, cols]], axis=0)
            v = point_ref[x, rows].reshape(share * ROWS, DEPTH) + dot(modes, back_ref[...], ((0,), (0,)))
            v = v.astype(BF)
            v = v * jax.nn.sigmoid(v * (jnp.asarray(a, BF) + jnp.asarray(a * 0.044715, BF) * (v * v)))
            stage[rows, x] = v.reshape(share, ROWS, DEPTH)
        copies.append(pltpu.make_async_copy(stage.at[rows], out_ref.at[rows], sems.at[q]))
        copies[-1].start()
    for copy in copies:
        copy.wait()


def call(kernel, name, args, outs, scratch=(), spaces=None):
    spaces = spaces or [pltpu.VMEM] * len(args)
    args = [x if s is pl.ANY else pltpu.with_memory_space_constraint(x, s) for x, s in zip(args, spaces)]
    spec = lambda s: pl.BlockSpec(memory_space=pl.ANY if s is pltpu.HBM else s)
    return pl.pallas_call(
        kernel,
        out_shape=outs,
        in_specs=[spec(s) for s in spaces],
        out_specs=jax.tree.map(lambda o: spec(o.memory_space), outs),
        scratch_shapes=list(scratch),
        compiler_params=pltpu.CompilerParams(vmem_limit_bytes=12 * 2**20),
        name=name,
    )(*args)


def shards(field, spectral_weight, point_weight, bias):
    front, across, along, back, planes = (jnp.asarray(t) for t in tables())
    swap = [(0, 1), (1, 0)]
    vm = lambda *shape, dtype=BF: pltpu.VMEM(shape, dtype)
    dma = pltpu.SemaphoreType.DMA

    own, send, back, planes, along, grid = call(
        analysis_kernel,
        "analysis",
        (field, front, across, back, planes, along, spectral_weight),
        (vm(128, 512), vm(192, 512), vm(48, DEPTH), vm(256, 256), vm(32, 32), vm(C, X, ROWS, DEPTH)),
        (
            vm(X * DEPTH, 256),
            vm(DEPTH, 256),
            vm(X, 256, dtype=F32),
            vm(4, 8, 1024),
            dma,
            dma((6,)),
        ),
        (pltpu.HBM,) * 7,
    )
    recv = lax.ppermute(send, "c", swap)
    wy, order, kron, shift = call(
        tables_kernel,
        "tables",
        (along, point_weight, bias.reshape(1, 32)),
        (vm(512, 512), vm(256, 256), vm(256, 256), vm(16, 512)),
    )
    parts, peer_weight = call(
        rows_kernel,
        "rows",
        (own, recv, wy, order),
        (vm(1024, 128), vm(64, 512)),
    )
    parts = lax.all_to_all(parts.reshape(128, 8, 128), ("x", "z", "y"), 0, 0, axis_index_groups=GROUP, tiled=True)
    mixed = call(
        mix_kernel,
        "mix",
        (parts.reshape(1024, 128), spectral_weight, peer_weight),
        vm(1024, 128),
    )
    modes = lax.all_to_all(mixed.reshape(128, 8, 128), ("x", "z", "y"), 0, 0, axis_index_groups=GROUP, tiled=True)
    own, send = call(
        modes_kernel,
        "modes",
        (modes.reshape(1024, 128), wy, planes),
        (vm(128, 512), vm(128, 512)),
    )
    recv = lax.ppermute(send, "c", swap)
    point = call(
        point_kernel,
        "point",
        (grid, kron, own),
        vm(X, C, ROWS, DEPTH, dtype=F32),
        (),
        (pltpu.VMEM, pltpu.VMEM, pl.ANY),
    )
    return call(
        grid_kernel,
        "grid",
        (point, own, recv, shift, back),
        pltpu.HBM((C, X, ROWS, DEPTH), BF),
        (vm(C, X, ROWS, DEPTH), dma((CHUNKS,))),
    )


def solution(mesh):
    fine = Mesh(mesh.devices.reshape(DZ, DY, DC, DX), ("z", "y", "c", "x"))
    return jax.shard_map(
        shards,
        mesh=fine,
        in_specs=(P(None, None, ("z", "y", "c"), "x"), P(("z", "y", "c"), "x", None), P(), P()),
        out_specs=P(None, None, ("z", "y", "c"), "x"),
        check_vma=False,
    )
```

```python
import math

import jax
import jax.numpy as jnp
import ml_dtypes
import numpy as np
from jax import lax
from jax.experimental import pallas as pl
from jax.experimental.pallas import tpu as pltpu
from jax.sharding import Mesh
from jax.sharding import PartitionSpec as P

C, X, K, N = 32, 8, 32, 1024
DZ, DY, DC, DX = 8, 4, 2, 4
ROWS = N // (DZ * DY * DC)
DEPTH = N // DX
CHUNKS = 4
BF = jnp.bfloat16
F32 = jnp.float32


def hops(chip):
    return sum(min(at, size - at) for at, size in zip(chip, (DX, DZ, DY)))


CHIPS = [(x, z, y) for x in range(DX) for z in range(DZ) for y in range(DY)]
ORDER = sorted(CHIPS, key=lambda chip: (chip != (DX // 2, DZ // 2, DY // 2), hops(chip)))
SLOT = {chip: at for at, chip in enumerate(ORDER)}
GROUP = [[CHIPS.index(chip) for chip in ORDER]]


def cosines(count, length, norm):
    modes = np.arange(count, dtype=np.float64)[:, None]
    spots = np.arange(length, dtype=np.float64)[None, :]
    value = norm * np.cos(np.pi * modes * (spots + 0.5) / length)
    value[0] *= math.sqrt(0.5)
    return value


def tables():
    ax = cosines(X, X, math.sqrt(2.0 / X))
    ay = cosines(K, N, math.sqrt(2.0 / N))
    az = cosines(K, N, math.sqrt(2.0 / N)).astype(ml_dtypes.bfloat16).astype(np.float64)
    sz = cosines(K, N, math.sqrt(2.0 / K))
    kq, kx, i = np.meshgrid(np.arange(4), np.arange(DX), np.arange(X), indexing="ij")
    front = np.zeros((DX, DC, DEPTH, 2, 128))
    for core in range(DC):
        for h in range(2):
            k = (kx * 8 + (core ^ h) * 4 + kq).reshape(-1)
            front[:, core, :, h] = az[k].reshape(128, DX, DEPTH).transpose(1, 2, 0)
    across = np.tile(ax[i.reshape(-1)].T, (1, 2))
    along = np.zeros((DZ * DY * DC, 32, 32))
    for dev in range(DZ * DY * DC):
        core = dev % 2
        spots = np.concatenate([dev * ROWS + np.arange(ROWS), (dev ^ 1) * ROWS + np.arange(ROWS)])
        octet = np.concatenate([core * 4 + np.arange(4), (1 - core) * 4 + np.arange(4)])
        j = (np.arange(4)[:, None] * 8 + octet[None, :]).reshape(-1)
        along[dev] = ay[j][:, spots].T
    back = np.zeros((DX * DC, 48, DEPTH))
    q2, x2 = np.meshgrid(np.arange(4), np.arange(DX), indexing="ij")
    for chip in range(DX):
        for core in range(DC):
            own = (x2 * 8 + core * 4 + q2).reshape(-1)
            other = (x2 * 8 + (1 - core) * 4 + q2).reshape(-1)
            part = slice(chip * DEPTH, (chip + 1) * DEPTH)
            back[chip * 2 + core, :16] = sz[own][:, part]
            back[chip * 2 + core, 16:32] = sz[other][:, part]
            back[chip * 2 + core, 32:35] = 1.0
    planes = np.zeros((2, X, 4, DX, DX, X, 2, 4))
    for g in range(2):
        for q in range(4):
            for chip in range(DX):
                planes[g, :, q, chip, chip, :, g, q] = ax.T * math.sqrt(N / K)
    bf = ml_dtypes.bfloat16
    return (
        front.reshape(DX, DC, DEPTH, 256).astype(bf),
        across.astype(np.float32),
        along.astype(bf),
        back.astype(bf),
        planes.reshape(256, 256).astype(bf),
    )


def dot(a, b, dims=((1,), (0,))):
    return lax.dot_general(a, b, (dims, ((), ())), preferred_element_type=F32)


def iota(shape, dim):
    return lax.broadcasted_iota(jnp.int32, shape, dim)


def ones_where(condition):
    return jnp.where(condition, 1.0, 0.0).astype(BF)


def at_chip():
    return lax.axis_index("x")


def at_core():
    return lax.axis_index("c")


def at_rows():
    return (lax.axis_index("z") * DY + lax.axis_index("y")) * DC + lax.axis_index("c")


def analysis_kernel(
    field, front, across, back, planes, along, weight,
    own, send, back_out, planes_out, along_out, grid,
    weights, base, vectors, mixing, field_sem, sems,
):
    copy = pltpu.make_async_copy(field, grid, field_sem)
    loads = [
        pltpu.make_async_copy(source, target, sems.at[at])
        for at, (source, target) in enumerate(
            (
                (front.at[at_chip(), at_core()], base),
                (across, vectors),
                (weight, mixing),
                (back.at[at_chip() * DC + at_core()], back_out),
                (planes, planes_out),
                (along.at[at_rows()], along_out),
            )
        )
    ]
    loads[0].start()
    loads[1].start()
    copy.start()
    for load in loads[2:]:
        load.start()
    loads[0].wait()
    loads[1].wait()
    wide = base[...].astype(F32)
    for x in range(X):
        weights[pl.ds(x * DEPTH, DEPTH), :] = (wide * vectors[pl.ds(x, 1), :]).astype(BF)
    for load in loads[2:]:
        load.wait()
    given = mixing[...].reshape(32, 1024)
    send[128:160, :] = given[:, :512]
    send[160:192, :] = given[:, 512:]
    copy.wait()
    lhs = jnp.concatenate([grid[:, x].reshape(C * ROWS, DEPTH) for x in range(X)], axis=1)
    res = dot(lhs, weights[...]).T.astype(BF)
    own[...] = res[:128]
    send[:128, :] = res[128:]


def tables_kernel(along_ref, point_ref, bias_ref, wy, order_ref, kron_ref, shift_ref):
    to, source = iota((256, 256), 0), iota((256, 256), 1)
    order_ref[...] = ones_where(source == (to // 4 % 2) * 128 + (to % 4) * 32 + to // 8)
    e1 = ones_where(iota((256, 32), 0) // 8 == iota((256, 32), 1))
    e2 = ones_where(iota((32, 256), 0) == iota((32, 256), 1) // 8)
    wide = dot(dot(e1, point_ref[...], ((1,), (1,))).astype(BF), e2)
    same = iota((256, 256), 0) % 8 == iota((256, 256), 1) % 8
    kron_ref[...] = jnp.where(same, wide, 0.0).astype(BF)
    b = jnp.broadcast_to(bias_ref[...], (16, 32))
    b1 = b.astype(BF).astype(F32)
    b2 = (b - b1).astype(BF).astype(F32)
    b3 = b - b1 - b2
    row = iota((16, 32), 0)
    parts = jnp.where(row == 0, b1, jnp.where(row == 1, b2, jnp.where(row == 2, b3, 0.0)))
    e3 = ones_where(iota((32, 512), 0) == iota((32, 512), 1) // 16)
    shift_ref[...] = dot(parts.astype(BF), e3).astype(BF)
    p1 = ones_where(
        (iota((512, 32), 0) // 256 == iota((512, 32), 1) // 16)
        & (iota((512, 32), 0) % 16 == iota((512, 32), 1) % 16)
    )
    p2 = ones_where(
        (iota((32, 512), 0) // 8 == iota((32, 512), 1) // 128)
        & (iota((32, 512), 0) % 8 == iota((32, 512), 1) % 8)
    )
    same = (iota((512, 512), 0) // 16) % 16 == (iota((512, 512), 1) // 8) % 16
    full = dot(dot(p1, along_ref[...]).astype(BF), p2)
    wy[...] = jnp.where(same, full, 0.0).astype(BF)


def rows_kernel(own_ref, recv_ref, wy_ref, order_ref, out_ref, peer_out):
    halves = []
    for g in range(2):
        part = pl.ds(g * 256, 256)
        halves.append(jnp.concatenate([own_ref[:, part], recv_ref[:128, part]], axis=1))
    lhs = dot(order_ref[...], jnp.concatenate(halves, axis=0)).astype(BF)
    res = dot(lhs, wy_ref[...])
    for to in range(32):
        for joct in range(4):
            out_ref[pl.ds(SLOT[to // 8, to % 8, joct] * 8, 8), :] = res[
                to * 8 : (to + 1) * 8, joct * 128 : (joct + 1) * 128
            ].astype(BF)
    peer_out[...] = recv_ref[128:192, :]


def mix_kernel(parts_ref, weight_ref, peer_ref, out_ref):
    core = at_core()
    s = jnp.sum(parts_ref[...].astype(F32).reshape(128, 8, 128), axis=0)
    row = iota((8, 128), 0)
    turned = pltpu.roll(s, 4, 0)
    s8 = jnp.concatenate([jnp.where(row < 4, s, turned), jnp.where(row < 4, turned, s)], axis=1)
    s64 = jnp.concatenate([s8] * 8, axis=0)
    row = iota((64, 256), 0)
    keep = (iota((64, 256), 1) % 8 == row // 8) & ((row % 8) // 4 == core)
    s64 = jnp.where(keep, s64, 0.0)
    high = s64.astype(BF)
    low = (s64 - high.astype(F32)).astype(BF)
    parts = jnp.concatenate([high, low], axis=0)
    spread = ones_where(iota((128, 512), 0) // 8 == iota((128, 512), 1) // 32)
    peer = jnp.concatenate([peer_ref[:32, :], peer_ref[32:, :]], axis=1)
    weight = jnp.concatenate([weight_ref[...].reshape(32, 1024), peer], axis=0).astype(F32)
    total = jnp.zeros((64, 128), F32)
    for g in range(2):
        wide = dot(parts[:, g * 128 : (g + 1) * 128], spread)
        prod = (wide[:64] + wide[64:]) * weight[:, g * 512 : (g + 1) * 512]
        for part in range(4):
            total = total + prod[:, part * 128 : (part + 1) * 128]
    total = total + pltpu.roll(total, 64, 1)
    total = total + pltpu.roll(total, 32, 1)
    mixed = total.astype(BF)
    q, col = iota((128, 256), 0), iota((128, 256), 1)
    place = ones_where(q == (col // 128) * 16 + (col % 128) // 8)
    placed = dot(mixed, place)
    placed = jnp.where(iota((64, 256), 1) % 8 == iota((64, 256), 0) // 8, placed, 0.0)
    both = placed[:8]
    for j in range(1, 8):
        both = both + placed[j * 8 : (j + 1) * 8]
    both = both + pltpu.roll(both, 4, 0)
    out = jnp.where(iota((8, 128), 0) < 4, both[:, :128], both[:, 128:]).astype(BF)
    out_ref[...] = jnp.broadcast_to(out[None], (128, 8, 128)).reshape(1024, 128)


def modes_kernel(modes_ref, wy_ref, planes_ref, own_ref, send_ref):
    rows = []
    for to in range(32):
        cols = [modes_ref[pl.ds(SLOT[to // 8, to % 8, joct] * 8, 8), :] for joct in range(4)]
        rows.append(jnp.concatenate(cols, axis=1))
    res = dot(jnp.concatenate(rows, axis=0), wy_ref[...], ((1,), (1,))).astype(BF)
    res = dot(planes_ref[...], res).astype(BF)
    for g in range(2):
        part = pl.ds(g * 256, 256)
        own_ref[:, part] = res[g * 128 : (g + 1) * 128, :256]
        send_ref[:, part] = res[g * 128 : (g + 1) * 128, 256:]


def point_kernel(grid_ref, kron_ref, after_ref, out_ref):
    for x in range(X):
        for half in range(2):
            part = slice(half * 8, half * 8 + 8)
            res = dot(kron_ref[...], grid_ref[:, x, part, :].reshape(C * 8, DEPTH))
            out_ref[x, :, part, :] = res.reshape(C, 8, DEPTH)


def grid_kernel(point_ref, own_ref, recv_ref, shift_ref, back_ref, out_ref, stage, sems):
    a = 2.0 * math.sqrt(2.0 / math.pi)
    share = C // CHUNKS
    copies = []
    for q in range(CHUNKS):
        cols = pl.ds(q * share * ROWS, share * ROWS)
        rows = pl.ds(q * share, share)
        for x in range(X):
            part = pl.ds(x * 16, 16)
            modes = jnp.concatenate([own_ref[part, cols], recv_ref[part, cols], shift_ref[:, cols]], axis=0)
            v = point_ref[x, rows].reshape(share * ROWS, DEPTH) + dot(modes, back_ref[...], ((0,), (0,)))
            v = v.astype(BF)
            v = v * jax.nn.sigmoid(v * (jnp.asarray(a, BF) + jnp.asarray(a * 0.044715, BF) * (v * v)))
            stage[rows, x] = v.reshape(share, ROWS, DEPTH)
        copies.append(pltpu.make_async_copy(stage.at[rows], out_ref.at[rows], sems.at[q]))
        copies[-1].start()
    for copy in copies:
        copy.wait()


def call(kernel, name, args, outs, scratch=(), spaces=None):
    spaces = spaces or [pltpu.VMEM] * len(args)
    args = [x if s is pl.ANY else pltpu.with_memory_space_constraint(x, s) for x, s in zip(args, spaces)]
    spec = lambda s: pl.BlockSpec(memory_space=pl.ANY if s is pltpu.HBM else s)
    return pl.pallas_call(
        kernel,
        out_shape=outs,
        in_specs=[spec(s) for s in spaces],
        out_specs=jax.tree.map(lambda o: spec(o.memory_space), outs),
        scratch_shapes=list(scratch),
        compiler_params=pltpu.CompilerParams(vmem_limit_bytes=12 * 2**20),
        name=name,
    )(*args)


def shards(field, spectral_weight, point_weight, bias):
    front, across, along, back, planes = (jnp.asarray(t) for t in tables())
    swap = [(0, 1), (1, 0)]
    vm = lambda *shape, dtype=BF: pltpu.VMEM(shape, dtype)
    dma = pltpu.SemaphoreType.DMA

    own, send, back, planes, along, grid = call(
        analysis_kernel,
        "analysis",
        (field, front, across, back, planes, along, spectral_weight),
        (vm(128, 512), vm(192, 512), vm(48, DEPTH), vm(256, 256), vm(32, 32), vm(C, X, ROWS, DEPTH)),
        (
            vm(X * DEPTH, 256),
            vm(DEPTH, 256),
            vm(X, 256, dtype=F32),
            vm(4, 8, 1024),
            dma,
            dma((6,)),
        ),
        (pltpu.HBM,) * 7,
    )
    recv = lax.ppermute(send, "c", swap)
    wy, order, kron, shift = call(
        tables_kernel,
        "tables",
        (along, point_weight, bias.reshape(1, 32)),
        (vm(512, 512), vm(256, 256), vm(256, 256), vm(16, 512)),
    )
    parts, peer_weight = call(
        rows_kernel,
        "rows",
        (own, recv, wy, order),
        (vm(1024, 128), vm(64, 512)),
    )
    parts = lax.all_to_all(parts.reshape(128, 8, 128), ("x", "z", "y"), 0, 0, axis_index_groups=GROUP, tiled=True)
    mixed = call(
        mix_kernel,
        "mix",
        (parts.reshape(1024, 128), spectral_weight, peer_weight),
        vm(1024, 128),
    )
    modes = lax.all_to_all(mixed.reshape(128, 8, 128), ("x", "z", "y"), 0, 0, axis_index_groups=GROUP, tiled=True)
    own, send = call(
        modes_kernel,
        "modes",
        (modes.reshape(1024, 128), wy, planes),
        (vm(128, 512), vm(128, 512)),
    )
    recv = lax.ppermute(send, "c", swap)
    point = call(
        point_kernel,
        "point",
        (grid, kron, own),
        vm(X, C, ROWS, DEPTH, dtype=F32),
        (),
        (pltpu.VMEM, pltpu.VMEM, pl.ANY),
    )
    return call(
        grid_kernel,
        "grid",
        (point, own, recv, shift, back),
        pltpu.HBM((C, X, ROWS, DEPTH), BF),
        (vm(C, X, ROWS, DEPTH), dma((CHUNKS,))),
    )


def solution(mesh):
    fine = Mesh(mesh.devices.reshape(DZ, DY, DC, DX), ("z", "y", "c", "x"))
    return jax.shard_map(
        shards,
        mesh=fine,
        in_specs=(P(None, None, ("z", "y", "c"), "x"), P(("z", "y", "c"), "x", None), P(), P()),
        out_specs=P(None, None, ("z", "y", "c"), "x"),
        check_vma=False,
    )
```

```python
import math

import jax
import jax.numpy as jnp
import ml_dtypes
import numpy as np
from jax import lax
from jax.experimental import pallas as pl
from jax.experimental.pallas import tpu as pltpu
from jax.sharding import Mesh
from jax.sharding import PartitionSpec as P

C, X, K, N = 32, 8, 32, 1024
DZ, DY, DC, DX = 8, 4, 2, 4
ROWS = N // (DZ * DY * DC)
DEPTH = N // DX
CHUNKS = 4
BF = jnp.bfloat16
F32 = jnp.float32


def hops(chip):
    return sum(min(at, size - at) for at, size in zip(chip, (DX, DZ, DY)))


CHIPS = [(x, z, y) for x in range(DX) for z in range(DZ) for y in range(DY)]
ORDER = sorted(CHIPS, key=lambda chip: (chip != (DX // 2, DZ // 2, DY // 2), hops(chip)))
SLOT = {chip: at for at, chip in enumerate(ORDER)}
GROUP = [[CHIPS.index(chip) for chip in ORDER]]


def cosines(count, length, norm):
    modes = np.arange(count, dtype=np.float64)[:, None]
    spots = np.arange(length, dtype=np.float64)[None, :]
    value = norm * np.cos(np.pi * modes * (spots + 0.5) / length)
    value[0] *= math.sqrt(0.5)
    return value


def tables():
    ax = cosines(X, X, math.sqrt(2.0 / X))
    ay = cosines(K, N, math.sqrt(2.0 / N))
    az = cosines(K, N, math.sqrt(2.0 / N)).astype(ml_dtypes.bfloat16).astype(np.float64)
    sz = cosines(K, N, math.sqrt(2.0 / K))
    kq, kx, i = np.meshgrid(np.arange(4), np.arange(DX), np.arange(X), indexing="ij")
    front = np.zeros((DX, DC, DEPTH, 2, 128))
    for core in range(DC):
        for h in range(2):
            k = (kx * 8 + (core ^ h) * 4 + kq).reshape(-1)
            front[:, core, :, h] = az[k].reshape(128, DX, DEPTH).transpose(1, 2, 0)
    across = np.tile(ax[i.reshape(-1)].T, (1, 2))
    along = np.zeros((DZ * DY * DC, 32, 32))
    for dev in range(DZ * DY * DC):
        core = dev % 2
        spots = np.concatenate([dev * ROWS + np.arange(ROWS), (dev ^ 1) * ROWS + np.arange(ROWS)])
        octet = np.concatenate([core * 4 + np.arange(4), (1 - core) * 4 + np.arange(4)])
        j = (np.arange(4)[:, None] * 8 + octet[None, :]).reshape(-1)
        along[dev] = ay[j][:, spots].T
    back = np.zeros((DX * DC, 48, DEPTH))
    q2, x2 = np.meshgrid(np.arange(4), np.arange(DX), indexing="ij")
    for chip in range(DX):
        for core in range(DC):
            own = (x2 * 8 + core * 4 + q2).reshape(-1)
            other = (x2 * 8 + (1 - core) * 4 + q2).reshape(-1)
            part = slice(chip * DEPTH, (chip + 1) * DEPTH)
            back[chip * 2 + core, :16] = sz[own][:, part]
            back[chip * 2 + core, 16:32] = sz[other][:, part]
            back[chip * 2 + core, 32:35] = 1.0
    planes = np.zeros((2, X, 4, DX, DX, X, 2, 4))
    for g in range(2):
        for q in range(4):
            for chip in range(DX):
                planes[g, :, q, chip, chip, :, g, q] = ax.T * math.sqrt(N / K)
    bf = ml_dtypes.bfloat16
    return (
        front.reshape(DX, DC, DEPTH, 256).astype(bf),
        across.astype(np.float32),
        along.astype(bf),
        back.astype(bf),
        planes.reshape(256, 256).astype(bf),
    )


def dot(a, b, dims=((1,), (0,))):
    return lax.dot_general(a, b, (dims, ((), ())), preferred_element_type=F32)


def iota(shape, dim):
    return lax.broadcasted_iota(jnp.int32, shape, dim)


def ones_where(condition):
    return jnp.where(condition, 1.0, 0.0).astype(BF)


def at_chip():
    return lax.axis_index("x")


def at_core():
    return lax.axis_index("c")


def at_rows():
    return (lax.axis_index("z") * DY + lax.axis_index("y")) * DC + lax.axis_index("c")


def analysis_kernel(
    field, front, across, back, planes, along, weight,
    own, send, back_out, planes_out, along_out, grid,
    weights, base, vectors, mixing, field_sem, sems,
):
    copy = pltpu.make_async_copy(field, grid, field_sem)
    loads = [
        pltpu.make_async_copy(source, target, sems.at[at])
        for at, (source, target) in enumerate(
            (
                (front.at[at_chip(), at_core()], base),
                (across, vectors),
                (weight, mixing),
                (back.at[at_chip() * DC + at_core()], back_out),
                (planes, planes_out),
                (along.at[at_rows()], along_out),
            )
        )
    ]
    loads[0].start()
    loads[1].start()
    copy.start()
    for load in loads[2:]:
        load.start()
    loads[0].wait()
    loads[1].wait()
    wide = base[...].astype(F32)
    for x in range(X):
        weights[pl.ds(x * DEPTH, DEPTH), :] = (wide * vectors[pl.ds(x, 1), :]).astype(BF)
    for load in loads[2:]:
        load.wait()
    given = mixing[...].reshape(32, 1024)
    send[128:160, :] = given[:, :512]
    send[160:192, :] = given[:, 512:]
    copy.wait()
    lhs = jnp.concatenate([grid[:, x].reshape(C * ROWS, DEPTH) for x in range(X)], axis=1)
    res = dot(lhs, weights[...]).T.astype(BF)
    own[...] = res[:128]
    send[:128, :] = res[128:]


def tables_kernel(along_ref, point_ref, bias_ref, wy, order_ref, kron_ref, shift_ref):
    to, source = iota((256, 256), 0), iota((256, 256), 1)
    order_ref[...] = ones_where(source == (to // 4 % 2) * 128 + (to % 4) * 32 + to // 8)
    e1 = ones_where(iota((256, 32), 0) // 8 == iota((256, 32), 1))
    e2 = ones_where(iota((32, 256), 0) == iota((32, 256), 1) // 8)
    wide = dot(dot(e1, point_ref[...], ((1,), (1,))).astype(BF), e2)
    same = iota((256, 256), 0) % 8 == iota((256, 256), 1) % 8
    kron_ref[...] = jnp.where(same, wide, 0.0).astype(BF)
    b = jnp.broadcast_to(bias_ref[...], (16, 32))
    b1 = b.astype(BF).astype(F32)
    b2 = (b - b1).astype(BF).astype(F32)
    b3 = b - b1 - b2
    row = iota((16, 32), 0)
    parts = jnp.where(row == 0, b1, jnp.where(row == 1, b2, jnp.where(row == 2, b3, 0.0)))
    e3 = ones_where(iota((32, 512), 0) == iota((32, 512), 1) // 16)
    shift_ref[...] = dot(parts.astype(BF), e3).astype(BF)
    p1 = ones_where(
        (iota((512, 32), 0) // 256 == iota((512, 32), 1) // 16)
        & (iota((512, 32), 0) % 16 == iota((512, 32), 1) % 16)
    )
    p2 = ones_where(
        (iota((32, 512), 0) // 8 == iota((32, 512), 1) // 128)
        & (iota((32, 512), 0) % 8 == iota((32, 512), 1) % 8)
    )
    same = (iota((512, 512), 0) // 16) % 16 == (iota((512, 512), 1) // 8) % 16
    full = dot(dot(p1, along_ref[...]).astype(BF), p2)
    wy[...] = jnp.where(same, full, 0.0).astype(BF)


def rows_kernel(own_ref, recv_ref, wy_ref, order_ref, out_ref, peer_out):
    halves = []
    for g in range(2):
        part = pl.ds(g * 256, 256)
        halves.append(jnp.concatenate([own_ref[:, part], recv_ref[:128, part]], axis=1))
    lhs = dot(order_ref[...], jnp.concatenate(halves, axis=0)).astype(BF)
    res = dot(lhs, wy_ref[...])
    for to in range(32):
        for joct in range(4):
            out_ref[pl.ds(SLOT[to // 8, to % 8, joct] * 8, 8), :] = res[
                to * 8 : (to + 1) * 8, joct * 128 : (joct + 1) * 128
            ].astype(BF)
    peer_out[...] = recv_ref[128:192, :]


def mix_kernel(parts_ref, weight_ref, peer_ref, out_ref):
    core = at_core()
    s = jnp.sum(parts_ref[...].astype(F32).reshape(128, 8, 128), axis=0)
    row = iota((8, 128), 0)
    turned = pltpu.roll(s, 4, 0)
    s8 = jnp.concatenate([jnp.where(row < 4, s, turned), jnp.where(row < 4, turned, s)], axis=1)
    s64 = jnp.concatenate([s8] * 8, axis=0)
    row = iota((64, 256), 0)
    keep = (iota((64, 256), 1) % 8 == row // 8) & ((row % 8) // 4 == core)
    s64 = jnp.where(keep, s64, 0.0)
    high = s64.astype(BF)
    low = (s64 - high.astype(F32)).astype(BF)
    parts = jnp.concatenate([high, low], axis=0)
    spread = ones_where(iota((128, 512), 0) // 8 == iota((128, 512), 1) // 32)
    peer = jnp.concatenate([peer_ref[:32, :], peer_ref[32:, :]], axis=1)
    weight = jnp.concatenate([weight_ref[...].reshape(32, 1024), peer], axis=0).astype(F32)
    total = jnp.zeros((64, 128), F32)
    for g in range(2):
        wide = dot(parts[:, g * 128 : (g + 1) * 128], spread)
        prod = (wide[:64] + wide[64:]) * weight[:, g * 512 : (g + 1) * 512]
        for part in range(4):
            total = total + prod[:, part * 128 : (part + 1) * 128]
    total = total + pltpu.roll(total, 64, 1)
    total = total + pltpu.roll(total, 32, 1)
    mixed = total.astype(BF)
    q, col = iota((128, 256), 0), iota((128, 256), 1)
    place = ones_where(q == (col // 128) * 16 + (col % 128) // 8)
    placed = dot(mixed, place)
    placed = jnp.where(iota((64, 256), 1) % 8 == iota((64, 256), 0) // 8, placed, 0.0)
    both = placed[:8]
    for j in range(1, 8):
        both = both + placed[j * 8 : (j + 1) * 8]
    both = both + pltpu.roll(both, 4, 0)
    out = jnp.where(iota((8, 128), 0) < 4, both[:, :128], both[:, 128:]).astype(BF)
    out_ref[...] = jnp.broadcast_to(out[None], (128, 8, 128)).reshape(1024, 128)


def modes_kernel(modes_ref, wy_ref, planes_ref, own_ref, send_ref):
    rows = []
    for to in range(32):
        cols = [modes_ref[pl.ds(SLOT[to // 8, to % 8, joct] * 8, 8), :] for joct in range(4)]
        rows.append(jnp.concatenate(cols, axis=1))
    res = dot(jnp.concatenate(rows, axis=0), wy_ref[...], ((1,), (1,))).astype(BF)
    res = dot(planes_ref[...], res).astype(BF)
    for g in range(2):
        part = pl.ds(g * 256, 256)
        own_ref[:, part] = res[g * 128 : (g + 1) * 128, :256]
        send_ref[:, part] = res[g * 128 : (g + 1) * 128, 256:]


def point_kernel(grid_ref, kron_ref, after_ref, out_ref):
    for x in range(X):
        for half in range(2):
            part = slice(half * 8, half * 8 + 8)
            res = dot(kron_ref[...], grid_ref[:, x, part, :].reshape(C * 8, DEPTH))
            out_ref[x, :, part, :] = res.reshape(C, 8, DEPTH)


def grid_kernel(point_ref, own_ref, recv_ref, shift_ref, back_ref, out_ref, stage, sems):
    a = 2.0 * math.sqrt(2.0 / math.pi)
    share = C // CHUNKS
    copies = []
    for q in range(CHUNKS):
        cols = pl.ds(q * share * ROWS, share * ROWS)
        rows = pl.ds(q * share, share)
        for x in range(X):
            part = pl.ds(x * 16, 16)
            modes = jnp.concatenate([own_ref[part, cols], recv_ref[part, cols], shift_ref[:, cols]], axis=0)
            v = point_ref[x, rows].reshape(share * ROWS, DEPTH) + dot(modes, back_ref[...], ((0,), (0,)))
            v = v.astype(BF)
            v = v * jax.nn.sigmoid(v * (jnp.asarray(a, BF) + jnp.asarray(a * 0.044715, BF) * (v * v)))
            stage[rows, x] = v.reshape(share, ROWS, DEPTH)
            if x % (X // 2) == X // 2 - 1:
                at = (rows, pl.ds(x - (X // 2 - 1), X // 2))
                copies.append(pltpu.make_async_copy(stage.at[at], out_ref.at[at], sems.at[len(copies)]))
                copies[-1].start()
    for copy in copies:
        copy.wait()


def call(kernel, name, args, outs, scratch=(), spaces=None):
    spaces = spaces or [pltpu.VMEM] * len(args)
    args = [x if s is pl.ANY else pltpu.with_memory_space_constraint(x, s) for x, s in zip(args, spaces)]
    spec = lambda s: pl.BlockSpec(memory_space=pl.ANY if s is pltpu.HBM else s)
    return pl.pallas_call(
        kernel,
        out_shape=outs,
        in_specs=[spec(s) for s in spaces],
        out_specs=jax.tree.map(lambda o: spec(o.memory_space), outs),
        scratch_shapes=list(scratch),
        compiler_params=pltpu.CompilerParams(vmem_limit_bytes=12 * 2**20),
        name=name,
    )(*args)


def shards(field, spectral_weight, point_weight, bias):
    front, across, along, back, planes = (jnp.asarray(t) for t in tables())
    swap = [(0, 1), (1, 0)]
    vm = lambda *shape, dtype=BF: pltpu.VMEM(shape, dtype)
    dma = pltpu.SemaphoreType.DMA

    own, send, back, planes, along, grid = call(
        analysis_kernel,
        "analysis",
        (field, front, across, back, planes, along, spectral_weight),
        (vm(128, 512), vm(192, 512), vm(48, DEPTH), vm(256, 256), vm(32, 32), vm(C, X, ROWS, DEPTH)),
        (
            vm(X * DEPTH, 256),
            vm(DEPTH, 256),
            vm(X, 256, dtype=F32),
            vm(4, 8, 1024),
            dma,
            dma((6,)),
        ),
        (pltpu.HBM,) * 7,
    )
    recv = lax.ppermute(send, "c", swap)
    wy, order, kron, shift = call(
        tables_kernel,
        "tables",
        (along, point_weight, bias.reshape(1, 32)),
        (vm(512, 512), vm(256, 256), vm(256, 256), vm(16, 512)),
    )
    parts, peer_weight = call(
        rows_kernel,
        "rows",
        (own, recv, wy, order),
        (vm(1024, 128), vm(64, 512)),
    )
    parts = lax.all_to_all(parts.reshape(128, 8, 128), ("x", "z", "y"), 0, 0, axis_index_groups=GROUP, tiled=True)
    mixed = call(
        mix_kernel,
        "mix",
        (parts.reshape(1024, 128), spectral_weight, peer_weight),
        vm(1024, 128),
    )
    modes = lax.all_to_all(mixed.reshape(128, 8, 128), ("x", "z", "y"), 0, 0, axis_index_groups=GROUP, tiled=True)
    own, send = call(
        modes_kernel,
        "modes",
        (modes.reshape(1024, 128), wy, planes),
        (vm(128, 512), vm(128, 512)),
    )
    recv = lax.ppermute(send, "c", swap)
    point = call(
        point_kernel,
        "point",
        (grid, kron, own),
        vm(X, C, ROWS, DEPTH, dtype=F32),
        (),
        (pltpu.VMEM, pltpu.VMEM, pl.ANY),
    )
    return call(
        grid_kernel,
        "grid",
        (point, own, recv, shift, back),
        pltpu.HBM((C, X, ROWS, DEPTH), BF),
        (vm(C, X, ROWS, DEPTH), dma((2 * CHUNKS,))),
    )


def solution(mesh):
    fine = Mesh(mesh.devices.reshape(DZ, DY, DC, DX), ("z", "y", "c", "x"))
    return jax.shard_map(
        shards,
        mesh=fine,
        in_specs=(P(None, None, ("z", "y", "c"), "x"), P(("z", "y", "c"), "x", None), P(), P()),
        out_specs=P(None, None, ("z", "y", "c"), "x"),
        check_vma=False,
    )
```

```python
import math

import jax
import jax.numpy as jnp
import ml_dtypes
import numpy as np
from jax import lax
from jax.experimental import pallas as pl
from jax.experimental.pallas import tpu as pltpu
from jax.sharding import Mesh
from jax.sharding import PartitionSpec as P

C, X, K, N = 32, 8, 32, 1024
DZ, DY, DC, DX = 8, 4, 2, 4
ROWS = N // (DZ * DY * DC)
DEPTH = N // DX
CHUNKS = 4
BF = jnp.bfloat16
F32 = jnp.float32


def hops(chip):
    return sum(min(at, size - at) for at, size in zip(chip, (DX, DZ, DY)))


CHIPS = [(x, z, y) for x in range(DX) for z in range(DZ) for y in range(DY)]
ORDER = sorted(CHIPS, key=lambda chip: (chip != (DX // 2, DZ // 2, DY // 2), hops(chip)))
SLOT = {chip: at for at, chip in enumerate(ORDER)}
GROUP = [[CHIPS.index(chip) for chip in ORDER]]


def cosines(count, length, norm):
    modes = np.arange(count, dtype=np.float64)[:, None]
    spots = np.arange(length, dtype=np.float64)[None, :]
    value = norm * np.cos(np.pi * modes * (spots + 0.5) / length)
    value[0] *= math.sqrt(0.5)
    return value


def tables():
    ax = cosines(X, X, math.sqrt(2.0 / X))
    ay = cosines(K, N, math.sqrt(2.0 / N))
    az = cosines(K, N, math.sqrt(2.0 / N)).astype(ml_dtypes.bfloat16).astype(np.float64)
    sz = cosines(K, N, math.sqrt(2.0 / K))
    kq, kx, i = np.meshgrid(np.arange(4), np.arange(DX), np.arange(X), indexing="ij")
    front = np.zeros((DX, DC, DEPTH, 2, 128))
    for core in range(DC):
        for h in range(2):
            k = (kx * 8 + (core ^ h) * 4 + kq).reshape(-1)
            front[:, core, :, h] = az[k].reshape(128, DX, DEPTH).transpose(1, 2, 0)
    across = np.tile(ax[i.reshape(-1)].T, (1, 2))
    along = np.zeros((DZ * DY * DC, 32, 32))
    for dev in range(DZ * DY * DC):
        core = dev % 2
        spots = np.concatenate([dev * ROWS + np.arange(ROWS), (dev ^ 1) * ROWS + np.arange(ROWS)])
        octet = np.concatenate([core * 4 + np.arange(4), (1 - core) * 4 + np.arange(4)])
        j = (np.arange(4)[:, None] * 8 + octet[None, :]).reshape(-1)
        along[dev] = ay[j][:, spots].T
    back = np.zeros((DX * DC, 48, DEPTH))
    q2, x2 = np.meshgrid(np.arange(4), np.arange(DX), indexing="ij")
    for chip in range(DX):
        for core in range(DC):
            own = (x2 * 8 + core * 4 + q2).reshape(-1)
            other = (x2 * 8 + (1 - core) * 4 + q2).reshape(-1)
            part = slice(chip * DEPTH, (chip + 1) * DEPTH)
            back[chip * 2 + core, :16] = sz[own][:, part]
            back[chip * 2 + core, 16:32] = sz[other][:, part]
            back[chip * 2 + core, 32:35] = 1.0
    planes = np.zeros((2, X, 4, DX, DX, X, 2, 4))
    for g in range(2):
        for q in range(4):
            for chip in range(DX):
                planes[g, :, q, chip, chip, :, g, q] = ax.T * math.sqrt(N / K)
    bf = ml_dtypes.bfloat16
    return (
        front.reshape(DX, DC, DEPTH, 256).astype(bf),
        across.astype(np.float32),
        along.astype(bf),
        back.astype(bf),
        planes.reshape(256, 256).astype(bf),
    )


def dot(a, b, dims=((1,), (0,))):
    return lax.dot_general(a, b, (dims, ((), ())), preferred_element_type=F32)


def iota(shape, dim):
    return lax.broadcasted_iota(jnp.int32, shape, dim)


def ones_where(condition):
    return jnp.where(condition, 1.0, 0.0).astype(BF)


def at_chip():
    return lax.axis_index("x")


def at_core():
    return lax.axis_index("c")


def at_rows():
    return (lax.axis_index("z") * DY + lax.axis_index("y")) * DC + lax.axis_index("c")


def analysis_kernel(
    field, front, across, back, planes, along, weight,
    own, send, back_out, planes_out, along_out, grid,
    weights, base, vectors, mixing, field_sem, sems,
):
    copy = pltpu.make_async_copy(field, grid, field_sem)
    loads = [
        pltpu.make_async_copy(source, target, sems.at[at])
        for at, (source, target) in enumerate(
            (
                (front.at[at_chip(), at_core()], base),
                (across, vectors),
                (weight, mixing),
                (back.at[at_chip() * DC + at_core()], back_out),
                (planes, planes_out),
                (along.at[at_rows()], along_out),
            )
        )
    ]
    loads[0].start()
    loads[1].start()
    copy.start()
    for load in loads[2:]:
        load.start()
    loads[0].wait()
    loads[1].wait()
    wide = base[...].astype(F32)
    for x in range(X):
        weights[pl.ds(x * DEPTH, DEPTH), :] = (wide * vectors[pl.ds(x, 1), :]).astype(BF)
    for load in loads[2:]:
        load.wait()
    given = mixing[...].reshape(32, 1024)
    send[128:160, :] = given[:, :512]
    send[160:192, :] = given[:, 512:]
    copy.wait()
    lhs = jnp.concatenate([grid[:, x].reshape(C * ROWS, DEPTH) for x in range(X)], axis=1)
    res = dot(lhs, weights[...]).T.astype(BF)
    own[...] = res[:128]
    send[:128, :] = res[128:]


def tables_kernel(along_ref, point_ref, bias_ref, wy, order_ref, kron_ref, shift_ref):
    to, source = iota((256, 256), 0), iota((256, 256), 1)
    order_ref[...] = ones_where(source == (to // 4 % 2) * 128 + (to % 4) * 32 + to // 8)
    e1 = ones_where(iota((256, 32), 0) // 8 == iota((256, 32), 1))
    e2 = ones_where(iota((32, 256), 0) == iota((32, 256), 1) // 8)
    wide = dot(dot(e1, point_ref[...], ((1,), (1,))).astype(BF), e2)
    same = iota((256, 256), 0) % 8 == iota((256, 256), 1) % 8
    kron_ref[...] = jnp.where(same, wide, 0.0).astype(BF)
    b = jnp.broadcast_to(bias_ref[...], (16, 32))
    b1 = b.astype(BF).astype(F32)
    b2 = (b - b1).astype(BF).astype(F32)
    b3 = b - b1 - b2
    row = iota((16, 32), 0)
    parts = jnp.where(row == 0, b1, jnp.where(row == 1, b2, jnp.where(row == 2, b3, 0.0)))
    e3 = ones_where(iota((32, 512), 0) == iota((32, 512), 1) // 16)
    shift_ref[...] = dot(parts.astype(BF), e3).astype(BF)
    p1 = ones_where(
        (iota((512, 32), 0) // 256 == iota((512, 32), 1) // 16)
        & (iota((512, 32), 0) % 16 == iota((512, 32), 1) % 16)
    )
    p2 = ones_where(
        (iota((32, 512), 0) // 8 == iota((32, 512), 1) // 128)
        & (iota((32, 512), 0) % 8 == iota((32, 512), 1) % 8)
    )
    same = (iota((512, 512), 0) // 16) % 16 == (iota((512, 512), 1) // 8) % 16
    full = dot(dot(p1, along_ref[...]).astype(BF), p2)
    wy[...] = jnp.where(same, full, 0.0).astype(BF)


def rows_kernel(own_ref, recv_ref, wy_ref, order_ref, out_ref, peer_out):
    halves = []
    for g in range(2):
        part = pl.ds(g * 256, 256)
        halves.append(jnp.concatenate([own_ref[:, part], recv_ref[:128, part]], axis=1))
    lhs = dot(order_ref[...], jnp.concatenate(halves, axis=0)).astype(BF)
    res = dot(lhs, wy_ref[...])
    for to in range(32):
        for joct in range(4):
            out_ref[pl.ds(SLOT[to // 8, to % 8, joct] * 8, 8), :] = res[
                to * 8 : (to + 1) * 8, joct * 128 : (joct + 1) * 128
            ].astype(BF)
    peer_out[...] = recv_ref[128:192, :]


def mix_kernel(parts_ref, weight_ref, peer_ref, out_ref):
    core = at_core()
    s = jnp.sum(parts_ref[...].astype(F32).reshape(128, 8, 128), axis=0)
    row = iota((8, 128), 0)
    turned = pltpu.roll(s, 4, 0)
    s8 = jnp.concatenate([jnp.where(row < 4, s, turned), jnp.where(row < 4, turned, s)], axis=1)
    s64 = jnp.concatenate([s8] * 8, axis=0)
    row = iota((64, 256), 0)
    keep = (iota((64, 256), 1) % 8 == row // 8) & ((row % 8) // 4 == core)
    s64 = jnp.where(keep, s64, 0.0)
    high = s64.astype(BF)
    low = (s64 - high.astype(F32)).astype(BF)
    parts = jnp.concatenate([high, low], axis=0)
    spread = ones_where(iota((128, 512), 0) // 8 == iota((128, 512), 1) // 32)
    peer = jnp.concatenate([peer_ref[:32, :], peer_ref[32:, :]], axis=1)
    weight = jnp.concatenate([weight_ref[...].reshape(32, 1024), peer], axis=0).astype(F32)
    total = jnp.zeros((64, 128), F32)
    for g in range(2):
        wide = dot(parts[:, g * 128 : (g + 1) * 128], spread)
        prod = (wide[:64] + wide[64:]) * weight[:, g * 512 : (g + 1) * 512]
        for part in range(4):
            total = total + prod[:, part * 128 : (part + 1) * 128]
    total = total + pltpu.roll(total, 64, 1)
    total = total + pltpu.roll(total, 32, 1)
    mixed = total.astype(BF)
    q, col = iota((128, 256), 0), iota((128, 256), 1)
    place = ones_where(q == (col // 128) * 16 + (col % 128) // 8)
    placed = dot(mixed, place)
    placed = jnp.where(iota((64, 256), 1) % 8 == iota((64, 256), 0) // 8, placed, 0.0)
    both = placed[:8]
    for j in range(1, 8):
        both = both + placed[j * 8 : (j + 1) * 8]
    both = both + pltpu.roll(both, 4, 0)
    out = jnp.where(iota((8, 128), 0) < 4, both[:, :128], both[:, 128:]).astype(BF)
    out_ref[...] = jnp.broadcast_to(out[None], (128, 8, 128)).reshape(1024, 128)


def modes_kernel(modes_ref, wy_ref, planes_ref, own_ref, send_ref):
    rows = []
    for to in range(32):
        cols = [modes_ref[pl.ds(SLOT[to // 8, to % 8, joct] * 8, 8), :] for joct in range(4)]
        rows.append(jnp.concatenate(cols, axis=1))
    res = dot(jnp.concatenate(rows, axis=0), wy_ref[...], ((1,), (1,))).astype(BF)
    res = dot(planes_ref[...], res).astype(BF)
    for g in range(2):
        part = pl.ds(g * 256, 256)
        own_ref[:, part] = res[g * 128 : (g + 1) * 128, :256]
        send_ref[:, part] = res[g * 128 : (g + 1) * 128, 256:]


def point_kernel(grid_ref, kron_ref, after_ref, out_ref):
    for x in range(X):
        for half in range(2):
            part = slice(half * 8, half * 8 + 8)
            res = dot(kron_ref[...], grid_ref[:, x, part, :].reshape(C * 8, DEPTH))
            out_ref[x, :, part, :] = res.reshape(C, 8, DEPTH)


def grid_kernel(point_ref, own_ref, recv_ref, shift_ref, back_ref, out_ref, stage, sems):
    a = 2.0 * math.sqrt(2.0 / math.pi)
    share = C // CHUNKS
    copies = []
    for q in range(CHUNKS):
        cols = pl.ds(q * share * ROWS, share * ROWS)
        rows = pl.ds(q * share, share)
        for x in range(X):
            part = pl.ds(x * 16, 16)
            modes = jnp.concatenate([own_ref[part, cols], recv_ref[part, cols], shift_ref[:, cols]], axis=0)
            v = point_ref[x, rows].reshape(share * ROWS, DEPTH) + dot(modes, back_ref[...], ((0,), (0,)))
            v = v.astype(BF)
            v = v * jax.nn.sigmoid(v * (jnp.asarray(a, BF) + jnp.asarray(a * 0.044715, BF) * (v * v)))
            stage[rows, x] = v.reshape(share, ROWS, DEPTH)
            if x % (X // 4) == X // 4 - 1:
                at = (rows, pl.ds(x - (X // 4 - 1), X // 4))
                copies.append(pltpu.make_async_copy(stage.at[at], out_ref.at[at], sems.at[len(copies)]))
                copies[-1].start()
    for copy in copies:
        copy.wait()


def call(kernel, name, args, outs, scratch=(), spaces=None):
    spaces = spaces or [pltpu.VMEM] * len(args)
    args = [x if s is pl.ANY else pltpu.with_memory_space_constraint(x, s) for x, s in zip(args, spaces)]
    spec = lambda s: pl.BlockSpec(memory_space=pl.ANY if s is pltpu.HBM else s)
    return pl.pallas_call(
        kernel,
        out_shape=outs,
        in_specs=[spec(s) for s in spaces],
        out_specs=jax.tree.map(lambda o: spec(o.memory_space), outs),
        scratch_shapes=list(scratch),
        compiler_params=pltpu.CompilerParams(vmem_limit_bytes=12 * 2**20),
        name=name,
    )(*args)


def shards(field, spectral_weight, point_weight, bias):
    front, across, along, back, planes = (jnp.asarray(t) for t in tables())
    swap = [(0, 1), (1, 0)]
    vm = lambda *shape, dtype=BF: pltpu.VMEM(shape, dtype)
    dma = pltpu.SemaphoreType.DMA

    own, send, back, planes, along, grid = call(
        analysis_kernel,
        "analysis",
        (field, front, across, back, planes, along, spectral_weight),
        (vm(128, 512), vm(192, 512), vm(48, DEPTH), vm(256, 256), vm(32, 32), vm(C, X, ROWS, DEPTH)),
        (
            vm(X * DEPTH, 256),
            vm(DEPTH, 256),
            vm(X, 256, dtype=F32),
            vm(4, 8, 1024),
            dma,
            dma((6,)),
        ),
        (pltpu.HBM,) * 7,
    )
    recv = lax.ppermute(send, "c", swap)
    wy, order, kron, shift = call(
        tables_kernel,
        "tables",
        (along, point_weight, bias.reshape(1, 32)),
        (vm(512, 512), vm(256, 256), vm(256, 256), vm(16, 512)),
    )
    parts, peer_weight = call(
        rows_kernel,
        "rows",
        (own, recv, wy, order),
        (vm(1024, 128), vm(64, 512)),
    )
    parts = lax.all_to_all(parts.reshape(128, 8, 128), ("x", "z", "y"), 0, 0, axis_index_groups=GROUP, tiled=True)
    mixed = call(
        mix_kernel,
        "mix",
        (parts.reshape(1024, 128), spectral_weight, peer_weight),
        vm(1024, 128),
    )
    modes = lax.all_to_all(mixed.reshape(128, 8, 128), ("x", "z", "y"), 0, 0, axis_index_groups=GROUP, tiled=True)
    own, send = call(
        modes_kernel,
        "modes",
        (modes.reshape(1024, 128), wy, planes),
        (vm(128, 512), vm(128, 512)),
    )
    recv = lax.ppermute(send, "c", swap)
    point = call(
        point_kernel,
        "point",
        (grid, kron, own),
        vm(X, C, ROWS, DEPTH, dtype=F32),
        (),
        (pltpu.VMEM, pltpu.VMEM, pl.ANY),
    )
    return call(
        grid_kernel,
        "grid",
        (point, own, recv, shift, back),
        pltpu.HBM((C, X, ROWS, DEPTH), BF),
        (vm(C, X, ROWS, DEPTH), dma((4 * CHUNKS,))),
    )


def solution(mesh):
    fine = Mesh(mesh.devices.reshape(DZ, DY, DC, DX), ("z", "y", "c", "x"))
    return jax.shard_map(
        shards,
        mesh=fine,
        in_specs=(P(None, None, ("z", "y", "c"), "x"), P(("z", "y", "c"), "x", None), P(), P()),
        out_specs=P(None, None, ("z", "y", "c"), "x"),
        check_vma=False,
    )
```
